256 devices in a mesh: tp: 8 (over z_lo, core), seq: 32 (over x, y, z_hi).
Axes of the slice: x: 4, y: 4, z: 8 (z_hi: 2, z_lo: 4; z = z_hi * 4 + z_lo), core: 2. Of those that a mesh axis runs over, the one named last changes fastest.
Arguments:
- queries: bfloat16 [4096, 8192], P('seq', 'tp'), may hold values from -184 to 184
- cache_keys: bfloat16 [8192, 1024], P('seq', 'tp'), may hold values from -6.2 to 6.2
- prefix_values: bfloat16 [8192, 1024], P('seq', 'tp'), may hold values from -6 to 6
- slab_key_rows: bfloat16 [4096, 1024], P('seq', 'tp'), may hold values from -6 to 6
- slab_value_rows: bfloat16 [4096, 1024], P('seq', 'tp'), may hold values from -6 to 6
- student_log_decay: float32 [64, 4096], P('tp', 'seq'), may hold values from 0 to 1
- student_step: float32 [64, 4096], P('tp', 'seq'), may hold values from 0.002 to 0.02
- student_skip_weight: float32 [64], P('tp'), may hold values from 0.1 to 0.5
- out_weight: bfloat16 [8192, 8192], P('tp', 'seq'), may hold values from -0.0625 to 0.0625
Outputs:
- gap_out: bfloat16 [4096, 8192], P('seq', 'tp')
The draws below stay inside these ranges and needn't reach their ends.
All inputs are finite; a program needn't handle non-finite values.
Results may differ from the reference program's by a relative error of at most 0.025.
Values may be sent and summed in bfloat16 or wider, within the bound.
No kernel may reach another device: no remote copies, remote signals or barrier semaphores. Data moves between devices by JAX's collectives and lax.ppermute only.
A program may use at most 128 MiB of HBM per device.

```python
import math
import jax
import jax.numpy as jnp
from jax import lax

D = 8192
ASKING_CHANNELS = 64
MEMORY_CHANNELS = 8
CHANNEL_DIM = 128
Q_DEV = 128
SCAN_BLOCK_SIZE = 64
TILE_SPAN = 4096
PREFIX_LENGTH = 8192


def base_cache_keys(key):
    return jnp.clip(jax.random.normal(key, (PREFIX_LENGTH, MEMORY_CHANNELS * CHANNEL_DIM), jnp.float32), -6.0, 6.0)


def draw_cache_keys(key, part):
    starting_shift = base_cache_keys(key)
    return starting_shift.astype(jnp.bfloat16)


def draw_queries(key, part):
    key = jax.random.fold_in(key, 23)
    first_key = jax.random.fold_in(key, 0)
    values_now = 2.5 * jnp.clip(jax.random.normal(first_key, (TILE_SPAN, ASKING_CHANNELS * CHANNEL_DIM), jnp.float32), -6.0, 6.0)
    return values_now.astype(jnp.bfloat16)


def draw_student_log_decay(key, part):
    key = jax.random.fold_in(key, 37)
    merged_lookup_vectors = jax.random.split(key, 7)
    order = jax.random.permutation(merged_lookup_vectors[0], ASKING_CHANNELS)
    gradual_version = order < ASKING_CHANNELS // 2
    slow_rate = jnp.exp(jax.random.uniform(merged_lookup_vectors[1], (ASKING_CHANNELS,), jnp.float32, jnp.log(0.1), jnp.log(0.4))) / TILE_SPAN
    fast_rate = jnp.exp(jax.random.uniform(merged_lookup_vectors[2], (ASKING_CHANNELS,), jnp.float32, jnp.log(1.0 / 40.0), jnp.log(1.0 / 20.0)))
    rate = jnp.where(gradual_version, slow_rate, fast_rate)
    device_factor = jnp.exp(jax.random.uniform(merged_lookup_vectors[3], (ASKING_CHANNELS, TILE_SPAN // Q_DEV, 1), jnp.float32, jnp.log(0.5), jnp.log(2.0)))
    device_factor = jnp.broadcast_to(device_factor, (ASKING_CHANNELS, TILE_SPAN // Q_DEV, Q_DEV)).reshape(ASKING_CHANNELS, TILE_SPAN)
    position_factor = jnp.exp(jax.random.uniform(merged_lookup_vectors[4], (ASKING_CHANNELS, TILE_SPAN), jnp.float32, jnp.log(0.7), jnp.log(1.4)))
    gentle_version = rate[:, None] * device_factor * position_factor
    spike_location = jax.random.randint(merged_lookup_vectors[5], (2,), 0, TILE_SPAN)
    spike_duration = jax.random.uniform(merged_lookup_vectors[6], (ASKING_CHANNELS, 2), jnp.float32, 0.22, 0.5)
    location_sequence = jnp.arange(TILE_SPAN)
    spike_collection = (location_sequence[None, :] == spike_location[0]) * spike_duration[:, 0:1] + (location_sequence[None, :] == spike_location[1]) * spike_duration[:, 1:2]
    return gentle_version + jnp.where(gradual_version[:, None], spike_collection, 0.0)


def block_scale(key, dims, pieces, least, high):
    def one(axis_at, parts):
        heights = jax.random.uniform(jax.random.fold_in(jax.random.fold_in(key, 6), axis_at), (parts,), jnp.float32, least / len(pieces), high / len(pieces))
        return jnp.repeat(jnp.exp(heights), dims[axis_at] // parts).reshape((-1,) + (1,) * (len(dims) - axis_at - 1))

    loudness = one(*pieces[0])
    for cut in pieces[1:]:
        loudness = loudness * one(*cut)
    return loudness


def normal_values(own_key, extent, deviation, reach, cuts=(), held_as=jnp.bfloat16):
    level = block_scale(own_key, extent, cuts, -0.22, 0.18) if cuts else 1.0
    values = jax.random.normal(own_key, extent, jnp.float32) * deviation * level
    return jnp.minimum(jnp.maximum(values, -reach), reach).astype(held_as)


def setup_inputs(seed: int = 0) -> dict:
    keys = jax.random.split(jax.random.key(seed), 10)
    return {
        "queries": draw_queries(jax.random.fold_in(keys[9], 71), 0),
        "cache_keys": draw_cache_keys(jax.random.fold_in(keys[9], 71), 0),
        "prefix_values": normal_values(keys[2], (PREFIX_LENGTH, MEMORY_CHANNELS * CHANNEL_DIM), 1.0, 6.0, ((0, 32), (1, 8))),
        "slab_key_rows": normal_values(keys[3], (TILE_SPAN, MEMORY_CHANNELS * CHANNEL_DIM), 1.0, 6.0, ((0, 32), (1, 8))),
        "slab_value_rows": normal_values(keys[4], (TILE_SPAN, MEMORY_CHANNELS * CHANNEL_DIM), 1.0, 6.0, ((0, 32), (1, 8))),
        "student_log_decay": draw_student_log_decay(jax.random.fold_in(keys[9], 71), 0),
        "student_step": jnp.clip(jnp.exp(math.log(0.02) - 2.30258502 * jax.random.uniform(keys[6], (ASKING_CHANNELS, TILE_SPAN), jnp.float32) ** block_scale(keys[6], (ASKING_CHANNELS, TILE_SPAN), ((0, 8), (1, 32)), -0.2, 0.2)), 0.002, 0.02),
        "student_skip_weight": jnp.clip(0.1 + 0.4 * jax.random.uniform(keys[7], (ASKING_CHANNELS,), jnp.float32) ** block_scale(keys[7], (ASKING_CHANNELS,), ((0, 8),), -0.2, 0.2), 0.1, 0.5),
        "out_weight": normal_values(keys[8], (ASKING_CHANNELS * CHANNEL_DIM, D), (ASKING_CHANNELS * CHANNEL_DIM) ** -0.5, 0.0625, ((0, 8), (1, 32))),
    }


highest = lax.Precision.HIGHEST


def scan_block(chain_state, inputs):
    query_part, key_part, value_part, decay_part, dt_part = inputs
    span = decay_part.shape[-1]
    inv_root = query_part.shape[-1] ** -0.5
    within = jnp.cumsum(decay_part, axis=-1)
    later = jnp.arange(span)[:, None] >= jnp.arange(span)[None, :]
    spread = within[..., :, None] - within[..., None, :]
    fade = jnp.where(later, jnp.exp(-jnp.where(later, spread, 0.0)), 0.0)
    affinity = jnp.einsum("ikgn,jkn->kgij", query_part, key_part, precision=highest) * inv_root
    weighted = affinity * fade * dt_part[..., None, :]
    inside = jnp.einsum("kgij,jkp->ikgp", weighted, value_part, precision=highest)
    entering = jnp.einsum("ikgn,kgnp->ikgp", query_part, chain_state, precision=highest)
    entering = entering * jnp.transpose(jnp.exp(-within) * inv_root, (2, 0, 1))[..., None]
    tail_weight = jnp.exp(within - within[..., -1:]) * dt_part
    added = jnp.einsum("jkn,kgj,jkp->kgnp", key_part, tail_weight, value_part, precision=highest)
    next_state = chain_state * jnp.exp(-within[..., -1])[..., None, None] + added
    return next_state, inside + entering


def reference(queries, cache_keys, prefix_values, slab_key_rows, slab_value_rows, student_log_decay, student_step, student_skip_weight, out_weight):
    query_group_count = ASKING_CHANNELS // MEMORY_CHANNELS
    inv_root = CHANNEL_DIM ** -0.5
    all_keys = jnp.concatenate([cache_keys, slab_key_rows], axis=0)
    all_values = jnp.concatenate([prefix_values, slab_value_rows], axis=0)
    query_rows = math.gcd(TILE_SPAN, 512)
    key_positions = jnp.arange(PREFIX_LENGTH + TILE_SPAN, dtype=jnp.int32)

    def single_head_attention(head_kv):
        key_head = lax.dynamic_slice_in_dim(all_keys, head_kv * CHANNEL_DIM, CHANNEL_DIM, 1).astype(jnp.float32)
        value_head = lax.dynamic_slice_in_dim(all_values, head_kv * CHANNEL_DIM, CHANNEL_DIM, 1).astype(jnp.float32)
        query_head = lax.dynamic_slice_in_dim(queries, head_kv * query_group_count * CHANNEL_DIM, query_group_count * CHANNEL_DIM, 1)
        query_head = query_head.reshape(TILE_SPAN, query_group_count, CHANNEL_DIM)

        def one_block(block_id):
            first = (block_id * query_rows).astype(jnp.int32)
            query_block = lax.dynamic_slice_in_dim(query_head, first, query_rows, 0).astype(jnp.float32)
            scores = jnp.einsum("qhd,kd->hqk", query_block, key_head) * inv_root
            query_positions = PREFIX_LENGTH + first + jnp.arange(query_rows, dtype=jnp.int32)
            allowed = key_positions[None, :] <= query_positions[:, None]
            masked = jnp.where(allowed[None], scores, -jnp.inf)
            row_max = jnp.max(masked, axis=-1, keepdims=True)
            expo = jnp.where(allowed[None], jnp.exp(masked - row_max), 0.0)
            totals = jnp.sum(expo, axis=-1)
            weights = expo.astype(jnp.bfloat16).astype(jnp.float32)
            summed = jnp.einsum("hqk,kd->qhd", weights, value_head)
            return (summed / jnp.transpose(totals)[..., None]).astype(jnp.bfloat16)

        blocks_out = lax.map(one_block, jnp.arange(TILE_SPAN // query_rows, dtype=jnp.int32))
        return blocks_out.reshape(TILE_SPAN, query_group_count * CHANNEL_DIM)

    head_outputs = lax.map(single_head_attention, jnp.arange(MEMORY_CHANNELS, dtype=jnp.int32))
    teacher_heads = jnp.transpose(head_outputs, (1, 0, 2)).reshape(TILE_SPAN, ASKING_CHANNELS * CHANNEL_DIM)

    block_list = TILE_SPAN // SCAN_BLOCK_SIZE
    query_wide = queries.astype(jnp.float32).reshape(TILE_SPAN, MEMORY_CHANNELS, query_group_count, CHANNEL_DIM)
    key_wide = slab_key_rows.astype(jnp.float32).reshape(TILE_SPAN, MEMORY_CHANNELS, CHANNEL_DIM)
    value_wide = slab_value_rows.astype(jnp.float32).reshape(TILE_SPAN, MEMORY_CHANNELS, CHANNEL_DIM)
    decay_table = student_log_decay.reshape(MEMORY_CHANNELS, query_group_count, TILE_SPAN)
    step_table = student_step.reshape(MEMORY_CHANNELS, query_group_count, TILE_SPAN)

    def split_rows(numeric_array):
        return numeric_array.reshape((block_list, SCAN_BLOCK_SIZE) + numeric_array.shape[1:])

    def split_time(numeric_array):
        return jnp.transpose(numeric_array.reshape(MEMORY_CHANNELS, query_group_count, block_list, SCAN_BLOCK_SIZE), (2, 0, 1, 3))

    initial_state = jnp.zeros((MEMORY_CHANNELS, query_group_count, CHANNEL_DIM, CHANNEL_DIM), jnp.float32)
    final_state, scan_result = lax.scan(scan_block, initial_state, (split_rows(query_wide), split_rows(key_wide), split_rows(value_wide), split_time(decay_table), split_time(step_table)))
    scan_result = scan_result.reshape(TILE_SPAN, MEMORY_CHANNELS, query_group_count, CHANNEL_DIM)
    student_table = scan_result + student_skip_weight.reshape(MEMORY_CHANNELS, query_group_count)[None, :, :, None] * value_wide[:, :, None, :]
    student_heads = student_table.reshape(TILE_SPAN, ASKING_CHANNELS * CHANNEL_DIM).astype(jnp.bfloat16)
    gap = (student_heads.astype(jnp.float32) - teacher_heads.astype(jnp.float32)).astype(jnp.bfloat16)
    return jnp.dot(gap, out_weight, preferred_element_type=jnp.float32).astype(jnp.bfloat16)
```

```python
import functools

import jax
import jax.numpy as jnp
import numpy as np
from jax import lax
from jax.experimental import pallas as pl
from jax.experimental.pallas import tpu as pltpu
from jax.sharding import Mesh
from jax.sharding import PartitionSpec as P

HEADS = 8
DIM = 128
ROWS = 128
CACHE = 256
META = 16
PACK = ROWS + META + CACHE
SCALE = DIM ** -0.5
SCALE2 = SCALE * 1.4426950408889634
LOW = -1e30
VMEM_LIMIT = 48 * 2**20
f32 = jnp.float32
bf16 = jnp.bfloat16
exact = lax.Precision.HIGHEST

whole = pl.BlockSpec(memory_space=pltpu.VMEM)
scalars = pl.BlockSpec(memory_space=pltpu.SMEM)


def params():
    return pltpu.CompilerParams(vmem_limit_bytes=VMEM_LIMIT)


def cost(flops, moved, exps=0):
    return pl.CostEstimate(flops=int(flops), bytes_accessed=int(moved), transcendentals=int(exps))


def dot_nt(a, b, precision=None):
    return lax.dot_general(
        a, b, (((1,), (1,)), ((), ())), preferred_element_type=f32, precision=precision
    )


def dot(a, b, precision=None):
    return jnp.dot(a, b, preferred_element_type=f32, precision=precision)


def iota(shape, axis):
    return lax.broadcasted_iota(jnp.int32, shape, axis)


def pack_kernel(key_ref, value_ref, cache_key_ref, cache_value_ref, decay_ref, step_ref, out_ref):
    decay = decay_ref[...]
    after = (iota((ROWS, ROWS), 0) > iota((ROWS, ROWS), 1)).astype(f32)
    to_end = dot(decay, after, exact)
    weight = jnp.exp(-to_end) * step_ref[...]
    total = jnp.broadcast_to(jnp.sum(decay, axis=1, keepdims=True), (HEADS, DIM))
    weight_high = weight.astype(bf16)
    total_high = total.astype(bf16)
    weight_low = (weight - weight_high.astype(f32)).astype(bf16)
    total_low = (total - total_high.astype(f32)).astype(bf16)
    out_ref[0, 0:ROWS, 0:DIM] = key_ref[...]
    out_ref[0, 0:ROWS, DIM:] = value_ref[...]
    out_ref[0, ROWS:ROWS + META, 0:DIM] = jnp.concatenate([weight_high, weight_low], 0)
    out_ref[0, ROWS:ROWS + META, DIM:] = jnp.concatenate([total_high, total_low], 0)
    out_ref[0, ROWS + META:, 0:DIM] = cache_key_ref[...]
    out_ref[0, ROWS + META:, DIM:] = cache_value_ref[...]


def pack(keys, values, cache_keys, cache_values, decay, step):
    return pl.pallas_call(
        pack_kernel,
        out_shape=jax.ShapeDtypeStruct((1, PACK, 2 * DIM), bf16),
        in_specs=[whole] * 6,
        out_specs=whole,
        compiler_params=params(),
        name="pack",
        cost_estimate=cost(1e6, 5e5),
    )(keys, values, cache_keys, cache_values, decay, step)


def own_kernel(query_ref, block_ref, decay_ref, step_ref, skip_ref, max_ref, acc_ref, inner_ref):
    slab_key = block_ref[0, 0:ROWS, 0:DIM]
    slab_value = block_ref[0, 0:ROWS, DIM:]
    keys = jnp.concatenate([slab_key, block_ref[0, ROWS + META:, 0:DIM]], 0)
    values = jnp.concatenate([slab_value, block_ref[0, ROWS + META:, DIM:]], 0)
    wide = jnp.concatenate([values, jnp.ones_like(values)], 1)
    row, col = iota((ROWS, ROWS), 0), iota((ROWS, ROWS), 1)
    causal = row >= col
    decay = decay_ref[...]
    upto = dot(decay, (row <= col).astype(f32), exact)
    upto_rows = dot_nt((row >= col).astype(f32), decay, exact)
    value_f32 = slab_value.astype(f32)
    for head in range(HEADS):
        query = query_ref[:, head * DIM:(head + 1) * DIM]
        scores = dot_nt(query, keys)
        slab_scores = scores[:, 0:ROWS]
        masked = jnp.concatenate([jnp.where(causal, slab_scores, LOW), scores[:, ROWS:]], 1)
        top = jnp.max(masked, axis=1, keepdims=True)
        weights = jnp.exp2((masked - top) * SCALE2)
        span = slice(head * ROWS, (head + 1) * ROWS)
        max_ref[span, :] = jnp.broadcast_to(top, (ROWS, DIM))
        acc_ref[span, :] = dot(weights.astype(bf16), wide)
        spread = upto_rows[:, head:head + 1] - upto[head:head + 1, :]
        fade = jnp.where(causal, jnp.exp(-jnp.where(causal, spread, 0.0)), 0.0)
        mixed = slab_scores * (fade * (step_ref[head:head + 1, :] * SCALE))
        inner_ref[:, head * DIM:(head + 1) * DIM] = (
            dot(mixed.astype(bf16), slab_value) + skip_ref[0, head] * value_f32
        )


def own_block(queries, block, decay, step, skip):
    return pl.pallas_call(
        own_kernel,
        out_shape=(
            jax.ShapeDtypeStruct((HEADS * ROWS, DIM), f32),
            jax.ShapeDtypeStruct((HEADS * ROWS, 2 * DIM), f32),
            jax.ShapeDtypeStruct((ROWS, HEADS * DIM), f32),
        ),
        in_specs=[whole] * 4 + [scalars],
        out_specs=(whole,) * 3,
        compiler_params=params(),
        name="own",
        cost_estimate=cost(3e8, 2.5e6, 5e5),
    )(queries, block, decay, step, skip)


def attend_kernel(counts, pair, id_ref, query_ref, *refs):
    pieces = refs[:len(counts)]
    max_in, acc_in, max_ref, acc_ref = refs[len(counts):]
    me = id_ref[0]
    max_ref[...] = max_in[...]
    acc_ref[...] = acc_in[...]

    def work(blocks):
        keys, values, bias = [], [], []
        for block, place in blocks:
            keys += [block[0:ROWS, 0:DIM], block[ROWS + META:, 0:DIM]]
            values += [block[0:ROWS, DIM:], block[ROWS + META:, DIM:]]
            bias.append(jnp.where(place < me, 0.0, LOW).astype(f32))
        keys = jnp.concatenate(keys, 0)
        values = jnp.concatenate(values, 0)
        wide = jnp.concatenate([values, jnp.ones_like(values)], 1)
        for head in range(HEADS):
            query = query_ref[:, head * DIM:(head + 1) * DIM]
            span = pl.ds(head * ROWS, ROWS)
            scores = dot_nt(query, keys)
            parts = []
            for i in range(len(blocks)):
                at = i * (ROWS + CACHE)
                parts += [scores[:, at:at + ROWS] + bias[i], scores[:, at + ROWS:at + ROWS + CACHE]]
            scores = jnp.concatenate(parts, 1)
            before = max_ref[span, :]
            top = jnp.maximum(before, jnp.max(scores, axis=1, keepdims=True))
            factor = jnp.exp2((before - top) * SCALE2)
            weights = jnp.exp2((scores - top[:, 0:1]) * SCALE2)
            max_ref[span, :] = top
            acc_ref[span, :] = acc_ref[span, :] * factor[:, 0:1] + dot(weights.astype(bf16), wide)

    first = 1
    for piece, count in zip(pieces, counts):
        size = min(pair, count)

        def step(i, carry, piece=piece, first=first, size=size):
            work([(piece.at[i * size + b], id_ref[first + i * size + b]) for b in range(size)])
            return carry

        lax.fori_loop(0, count // size, step, 0)
        first += count


def attend(ids, queries, pieces, running, pair, name):
    counts = tuple(p.shape[0] for p in pieces)
    blocks = sum(counts)
    elems = HEADS * ROWS * blocks * (ROWS + CACHE)
    return pl.pallas_call(
        functools.partial(attend_kernel, counts, pair),
        out_shape=(
            jax.ShapeDtypeStruct((HEADS * ROWS, DIM), f32),
            jax.ShapeDtypeStruct((HEADS * ROWS, 2 * DIM), f32),
        ),
        in_specs=[scalars] + [whole] * (3 + len(pieces)),
        out_specs=(whole,) * 2,
        input_output_aliases={2 + len(pieces): 0, 3 + len(pieces): 1},
        compiler_params=params(),
        name=name,
        cost_estimate=cost(elems * 768, 3e6 + blocks * 2e5, elems),
    )(ids, queries, *pieces, *running)


def finish_kernel(counts, id_ref, query_ref, decay_ref, inner_ref, acc_ref, *refs):
    pieces = refs[:len(counts)]
    out_ref, total_ref, fade_ref, state_ref = refs[len(counts):]
    me = id_ref[0]
    first = 1
    for piece, count in zip(pieces, counts):
        for b in range(count):
            total_ref[id_ref[first + b]] = (
                piece[b, ROWS:ROWS + HEADS, DIM:].astype(f32)
                + piece[b, ROWS + HEADS:ROWS + META, DIM:].astype(f32)
            )
        first += count
    places = sum(counts)

    def back(i, gone):
        place = places - 1 - i
        live = place < me
        fade_ref[place] = jnp.where(live, jnp.exp(-gone), 0.0)
        return gone + jnp.where(live, total_ref[place], 0.0)

    lax.fori_loop(0, places, back, jnp.zeros((HEADS, DIM), f32))

    state_ref[...] = jnp.zeros_like(state_ref)
    first = 1
    for piece, count in zip(pieces, counts):

        def step(i, carry, piece=piece, first=first):
            left, values = [], []
            for b in range(2):
                block = piece.at[i * 2 + b]
                place = id_ref[first + i * 2 + b]
                weight = (
                    block[ROWS:ROWS + HEADS, 0:DIM].astype(f32)
                    + block[ROWS + HEADS:ROWS + META, 0:DIM].astype(f32)
                ) * fade_ref[place]
                turned = block[0:ROWS, 0:DIM].astype(f32).T
                left.append(
                    jnp.concatenate(
                        [(turned * weight[h:h + 1, :]).astype(bf16) for h in range(HEADS)], 0
                    )
                )
                values.append(block[0:ROWS, DIM:])
            state_ref[...] += dot(jnp.concatenate(left, 1), jnp.concatenate(values, 0))
            return carry

        lax.fori_loop(0, count // 2, step, 0)
        first += count

    row, col = iota((ROWS, ROWS), 0), iota((ROWS, ROWS), 1)
    upto_rows = dot_nt((row >= col).astype(f32), decay_ref[...], exact)
    reach = jnp.exp(-upto_rows) * SCALE
    for head in range(HEADS):
        span = slice(head * DIM, (head + 1) * DIM)
        entering = dot(query_ref[:, span], state_ref[span, :].astype(bf16))
        student = inner_ref[:, span] + entering * reach[:, head:head + 1]
        teacher = acc_ref[span, 0:DIM] / acc_ref[span, DIM:DIM + 1]
        out_ref[:, span] = (
            student.astype(bf16).astype(f32) - teacher.astype(bf16).astype(f32)
        ).astype(bf16)


def finish(ids, queries, decay, inner, acc, pieces):
    counts = tuple(p.shape[0] for p in pieces)
    part = ROWS + META
    return pl.pallas_call(
        functools.partial(finish_kernel, counts),
        grid=(1,),
        out_shape=jax.ShapeDtypeStruct((ROWS, HEADS * DIM), bf16),
        in_specs=[scalars] + [whole] * 4
        + [pl.BlockSpec((c, part, 2 * DIM), lambda i: (0, 0, 0)) for c in counts],
        out_specs=whole,
        scratch_shapes=[
            pltpu.VMEM((sum(counts), HEADS, DIM), f32),
            pltpu.VMEM((sum(counts), HEADS, DIM), f32),
            pltpu.VMEM((HEADS * DIM, DIM), f32),
        ],
        compiler_params=params(),
        name="finish",
        cost_estimate=cost(1.5e9, 5e6, 1e5),
    )(ids, queries, decay, inner, acc, *pieces)


def project_kernel(order_ref, own_ref, other_ref, weight_ref, out_ref):
    weight = weight_ref[0]
    out_ref[0, 0:ROWS, :] = dot(own_ref[...], weight).astype(out_ref.dtype)
    out_ref[0, ROWS:, :] = dot(other_ref[...], weight).astype(out_ref.dtype)


def project(order, own, other, weight, dtype, name):
    groups = order.shape[0]
    depth, width = weight.shape[1:]
    return pl.pallas_call(
        project_kernel,
        grid_spec=pltpu.PrefetchScalarGridSpec(
            num_scalar_prefetch=1,
            grid=(groups,),
            in_specs=[
                pl.BlockSpec((ROWS, depth), lambda i, o: (0, 0)),
                pl.BlockSpec((ROWS, depth), lambda i, o: (0, 0)),
                pl.BlockSpec((1, depth, width), lambda i, o: (o[i], 0, 0)),
            ],
            out_specs=pl.BlockSpec((1, 2 * ROWS, width), lambda i, o: (i, 0, 0)),
        ),
        out_shape=jax.ShapeDtypeStruct((groups, 2 * ROWS, width), dtype),
        compiler_params=params(),
        name=name,
        cost_estimate=cost(2 * groups * 2 * ROWS * depth * width, groups * 1e6),
    )(order, own, other, weight)


Y = ("yh", "yl")
SEQ = ("x", "yh", "yl", "zh")
TP = ("zl", "c")


def moved(value, axis, by, count):
    return lax.ppermute(value, axis, [(i, (i + by) % count) for i in range(count)])


def shards(
    queries,
    cache_keys,
    prefix_values,
    slab_key_rows,
    slab_value_rows,
    student_log_decay,
    student_step,
    student_skip_weight,
    out_weight,
):
    x, yh, yl, zh = (lax.axis_index(a) for a in SEQ)
    zl, core = (lax.axis_index(a) for a in TP)
    y = yh * 2 + yl
    me = lax.axis_index(SEQ).astype(jnp.int32)

    def place(px, py, pz):
        return (px % 4) * 8 + (py % 4) * 2 + pz

    def ids(*places):
        return jnp.stack([jnp.asarray(p, jnp.int32) for p in (me, *places)])

    weight_all = lax.all_gather(out_weight, ("x", "yh", "zh"), axis=0)
    weight_all = weight_all.reshape(16, *out_weight.shape)

    skip = student_skip_weight.reshape(1, HEADS)
    own = pack(
        slab_key_rows, slab_value_rows, cache_keys, prefix_values, student_log_decay, student_step
    )
    other = moved(own, "zh", 1, 2)
    front = jnp.where(zh == 0, own, other)
    back = jnp.where(zh == 0, other, own)
    front_near = [moved(front, "x", by, 4) for by in (1, 3, 2)]
    back_near = [moved(back, Y, by, 4) for by in (1, 3, 2)]
    steps = (0, -1, 1, -2)
    front_all = jnp.concatenate([front] + front_near, 0)
    back_all = jnp.concatenate([back] + back_near, 0)

    front_up, front_down = moved(front_all, Y, 1, 4), moved(front_all, Y, 3, 4)
    back_up, back_down = moved(back_all, "x", 1, 4), moved(back_all, "x", 3, 4)
    front_far = [moved(front_up[:2], Y, 1, 4), moved(front_down[2:], Y, 3, 4)]
    back_far = [moved(back_up[:2], "x", 1, 4), moved(back_down[2:], "x", 3, 4)]

    def front_ids(dy, span=slice(0, 4)):
        return [place(x + s, y + dy, 0) for s in steps[span]]

    def back_ids(dx, span=slice(0, 4)):
        return [place(x + dx, y + s, 1) for s in steps[span]]

    max_run, acc_run, inner = own_block(
        queries, own, student_log_decay, student_step, skip
    )
    running = (max_run, acc_run)
    running = attend(ids(place(x, y, 1 - zh)), queries, [other], running, 1, "attend_zh")
    near_ids = front_ids(0)[1:] + back_ids(0)[1:]
    near = jnp.concatenate(front_near + back_near, 0)
    running = attend(ids(*near_ids), queries, [near], running, 3, "attend_near")
    next_ids = front_ids(-1) + front_ids(1) + back_ids(-1) + back_ids(1)
    next_pieces = [front_up, front_down, back_up, back_down]
    running = attend(ids(*next_ids), queries, next_pieces, running, 4, "attend_next")
    far_ids = (
        front_ids(-2, slice(0, 2)) + front_ids(2, slice(2, 4))
        + back_ids(-2, slice(0, 2)) + back_ids(2, slice(2, 4))
    )
    far_pieces = front_far + back_far
    running = attend(ids(*far_ids), queries, far_pieces, running, 4, "attend_far")
    gap = finish(
        ids(*(front_ids(0) + back_ids(0) + next_ids + far_ids)),
        queries,
        student_log_decay,
        inner,
        running[1],
        [front_all, back_all] + next_pieces + far_pieces,
    )

    gap_other = moved(gap, "yl", 1, 2)

    def order(half):
        return jnp.stack(
            [
                (((zl + s) % 4) * 4 + half * 2 + z).astype(jnp.int32)
                for s in range(4)
                for z in range(2)
            ]
        )

    sent = project(order(1 - core), gap, gap_other, weight_all, bf16, "project_sent")
    from_core = moved(sent, "c", 1, 2)
    kept = project(order(core), gap, gap_other, weight_all, f32, "project_kept")
    kept = kept.reshape(4, 2, 2 * ROWS, 256)
    from_core = from_core.reshape(4, 2, 2 * ROWS, 256)
    sums = kept + from_core.astype(f32)
    pieces = [moved(sums[s].astype(bf16), "zl", s, 4) for s in (1, 2, 3)]
    summed = sums[0] + pieces[0].astype(f32) + pieces[1].astype(f32) + pieces[2].astype(f32)
    mine = summed[:, :ROWS].astype(bf16)
    theirs = moved(summed[:, ROWS:].astype(bf16), "yl", 1, 2)
    low = jnp.where(yl == 0, mine, theirs)
    high = jnp.where(yl == 0, theirs, mine)
    return jnp.concatenate([low[0], low[1], high[0], high[1]], 1)


def solution(mesh):
    devices = np.asarray(mesh.devices).reshape(4, 2, 4, 2, 2, 2)
    split = Mesh(devices, TP + SEQ)
    rows = P(SEQ, TP)
    heads = P(TP, SEQ)
    return jax.shard_map(
        shards,
        mesh=split,
        in_specs=(rows, rows, rows, rows, rows, heads, heads, P(TP), heads),
        out_specs=rows,
        check_vma=False,
    )
```

```python
import functools

import jax
import jax.numpy as jnp
import numpy as np
from jax import lax
from jax.experimental import pallas as pl
from jax.experimental.pallas import tpu as pltpu
from jax.sharding import Mesh
from jax.sharding import PartitionSpec as P

HEADS = 8
DIM = 128
ROWS = 128
CACHE = 256
META = 16
PACK = ROWS + META + CACHE
SCALE = DIM ** -0.5
SCALE2 = SCALE * 1.4426950408889634
LOW = -1e30
VMEM_LIMIT = 48 * 2**20
f32 = jnp.float32
bf16 = jnp.bfloat16
exact = lax.Precision.HIGHEST

whole = pl.BlockSpec(memory_space=pltpu.VMEM)
scalars = pl.BlockSpec(memory_space=pltpu.SMEM)


def full(shape):
    return pl.BlockSpec(shape, lambda i: (0,) * len(shape))


def params():
    return pltpu.CompilerParams(vmem_limit_bytes=VMEM_LIMIT)


def cost(flops, moved, exps=0):
    return pl.CostEstimate(flops=int(flops), bytes_accessed=int(moved), transcendentals=int(exps))


def dot_nt(a, b, precision=None):
    return lax.dot_general(
        a, b, (((1,), (1,)), ((), ())), preferred_element_type=f32, precision=precision
    )


def dot(a, b, precision=None):
    return jnp.dot(a, b, preferred_element_type=f32, precision=precision)


def iota(shape, axis):
    return lax.broadcasted_iota(jnp.int32, shape, axis)


def pack_kernel(
    key_ref, value_ref, cache_key_ref, cache_value_ref, decay_in, step_in,
    out_ref, decay_ref, step_ref, sems,
):
    copies = [
        pltpu.make_async_copy(decay_in, decay_ref, sems.at[0]),
        pltpu.make_async_copy(step_in, step_ref, sems.at[1]),
        pltpu.make_async_copy(key_ref, out_ref.at[0, 0:ROWS, 0:DIM], sems.at[2]),
        pltpu.make_async_copy(value_ref, out_ref.at[0, 0:ROWS, DIM:], sems.at[3]),
        pltpu.make_async_copy(cache_key_ref, out_ref.at[0, ROWS + META:, 0:DIM], sems.at[4]),
        pltpu.make_async_copy(cache_value_ref, out_ref.at[0, ROWS + META:, DIM:], sems.at[5]),
    ]
    for copy in copies:
        copy.start()
    copies[0].wait()
    copies[1].wait()
    decay = decay_ref[...]
    after = (iota((ROWS, ROWS), 0) > iota((ROWS, ROWS), 1)).astype(f32)
    to_end = dot(decay, after, exact)
    weight = jnp.exp(-to_end) * step_ref[...]
    total = jnp.broadcast_to(jnp.sum(decay, axis=1, keepdims=True), (HEADS, DIM))
    out_ref[0, ROWS:ROWS + META, 0:DIM] = two_parts(weight)
    out_ref[0, ROWS:ROWS + META, DIM:] = two_parts(total)
    for copy in copies[2:]:
        copy.wait()


def two_parts(value):
    high = value.astype(bf16)
    low = (value - high.astype(f32)).astype(bf16)
    return jnp.concatenate([high, low], 0)


def joined(parts):
    return parts[0:HEADS].astype(f32) + parts[HEADS:META].astype(f32)


def pack(keys, values, cache_keys, cache_values, decay, step):
    small = jax.ShapeDtypeStruct((HEADS, ROWS), f32)
    return pl.pallas_call(
        pack_kernel,
        out_shape=(jax.ShapeDtypeStruct((1, PACK, 2 * DIM), bf16), small, small),
        in_specs=[pl.BlockSpec(memory_space=pltpu.HBM)] * 6,
        out_specs=(whole,) * 3,
        scratch_shapes=[pltpu.SemaphoreType.DMA((6,))],
        compiler_params=params(),
        name="pack",
        cost_estimate=cost(1e6, 5e5),
    )(keys, values, cache_keys, cache_values, decay, step)


def inner_kernel(query_ref, block_ref, decay_ref, step_ref, skip_ref, inner_ref):
    keys = block_ref[0, 0:ROWS, 0:DIM]
    values = block_ref[0, 0:ROWS, DIM:]
    row, col = iota((ROWS, ROWS), 0), iota((ROWS, ROWS), 1)
    causal = row >= col
    decay = decay_ref[...]
    upto = dot(decay, (row <= col).astype(f32), exact)
    upto_rows = dot_nt((row >= col).astype(f32), decay, exact)
    value_f32 = values.astype(f32)
    for head in range(HEADS):
        span = slice(head * DIM, (head + 1) * DIM)
        scores = dot_nt(query_ref[:, span], keys)
        spread = upto_rows[:, head:head + 1] - upto[head:head + 1, :]
        fade = jnp.where(causal, jnp.exp(-jnp.where(causal, spread, 0.0)), 0.0)
        mixed = scores * (fade * (step_ref[head:head + 1, :] * SCALE))
        inner_ref[:, span] = dot(mixed.astype(bf16), values) + skip_ref[0, head] * value_f32


def inner_block(queries, own, decay, step, skip):
    return pl.pallas_call(
        inner_kernel,
        out_shape=jax.ShapeDtypeStruct((ROWS, HEADS * DIM), f32),
        in_specs=[whole] * 4 + [scalars],
        out_specs=whole,
        compiler_params=params(),
        name="inner",
        cost_estimate=cost(1e8, 1.5e6, 2e5),
    )(queries, own, decay, step, skip)


GROUP = 8
SLAB_KEYS = GROUP * ROWS
KEYS = GROUP * (ROWS + CACHE)


def fades(total_ref, fade_ref, last):
    def back(i, gone):
        place = GROUP - 1 - i
        live = place < last
        fade_ref[place] = jnp.where(live, jnp.exp(-gone), 0.0)
        return gone + jnp.where(live, total_ref[place], 0.0)

    return lax.fori_loop(0, GROUP, back, jnp.zeros((HEADS, DIM), f32))


def state_of(keys_ref, wide_ref, weight_ref, fade_ref, state_ref):
    state_ref[...] = jnp.zeros_like(state_ref)

    def step(i, carry):
        left = []
        for b in range(2):
            g = i * 2 + b
            weight = weight_ref[g] * fade_ref[g]
            rows = pl.ds(pl.multiple_of(g * ROWS, ROWS), ROWS)
            turned = keys_ref[rows, :].astype(f32).T
            left.append(
                jnp.concatenate(
                    [(turned * weight[h:h + 1, :]).astype(bf16) for h in range(HEADS)], 0
                )
            )
        values = wide_ref[pl.ds(pl.multiple_of(i * 2 * ROWS, 2 * ROWS), 2 * ROWS), 0:DIM]
        state_ref[...] += dot(jnp.concatenate(left, 1), values)
        return carry

    lax.fori_loop(0, GROUP // 2, step, 0)


def collect_kernel(at_ref, *refs):
    pieces = refs[:4]
    keys_ref, wide_ref, sent_ref, weight_ref, total_ref, fade_ref, state_ref = refs[4:]
    wide_ref[:, DIM:] = jnp.ones((KEYS, DIM), bf16)
    for p in range(4):
        for z in range(2):
            piece = pieces[p]
            g = at_ref[p] * 2 + z
            slab = pl.ds(pl.multiple_of(g * ROWS, ROWS), ROWS)
            cache = pl.ds(SLAB_KEYS + (2 * p + z) * CACHE, CACHE)
            keys_ref[slab, :] = piece[z, 0:ROWS, 0:DIM]
            wide_ref[slab, 0:DIM] = piece[z, 0:ROWS, DIM:]
            keys_ref[cache, :] = piece[z, ROWS + META:, 0:DIM]
            wide_ref[cache, 0:DIM] = piece[z, ROWS + META:, DIM:]
            weight_ref[g] = joined(piece[z, ROWS:ROWS + META, 0:DIM])
            total_ref[g] = joined(piece[z, ROWS:ROWS + META, DIM:])
    group_total = fades(total_ref, fade_ref, GROUP)
    state_of(keys_ref, wide_ref, weight_ref, fade_ref, state_ref)
    sent_ref[0:HEADS * DIM, :] = state_ref[...].astype(bf16)
    sent_ref[HEADS * DIM:, :] = two_parts(group_total)


def collect(at, pieces):
    table = jax.ShapeDtypeStruct((GROUP, HEADS, DIM), f32)
    return pl.pallas_call(
        collect_kernel,
        out_shape=(
            jax.ShapeDtypeStruct((KEYS, DIM), bf16),
            jax.ShapeDtypeStruct((KEYS, 2 * DIM), bf16),
            jax.ShapeDtypeStruct((HEADS * DIM + META, DIM), bf16),
            table,
            table,
        ),
        in_specs=[scalars] + [whole] * 4,
        out_specs=(whole,) * 5,
        scratch_shapes=[
            pltpu.VMEM((GROUP, HEADS, DIM), f32),
            pltpu.VMEM((HEADS * DIM, DIM), f32),
        ],
        compiler_params=params(),
        name="collect",
        cost_estimate=cost(3e8, 6e6, 1e5),
    )(at, *pieces)


def attend_rows(query_ref, keys_ref, wide_ref, mask, heads_at_once, put):
    def step(i, carry):
        for b in range(heads_at_once):
            head = i * heads_at_once + b
            query = query_ref[:, pl.ds(pl.multiple_of(head * DIM, DIM), DIM)]
            scores = dot_nt(query, keys_ref[...])
            scores = jnp.concatenate([mask(scores[:, :SLAB_KEYS]), scores[:, SLAB_KEYS:]], 1)
            top = jnp.max(scores, axis=1, keepdims=True)
            weights = jnp.exp2((scores - top) * SCALE2).astype(bf16)
            summed = dot(weights, wide_ref[...])
            total = summed[:, DIM:]
            put(head, summed[:, :DIM] / total, top * SCALE2 + jnp.log2(total))
        return carry

    lax.fori_loop(0, HEADS // heads_at_once, step, 0)


def others_kernel(at_ref, query_ref, keys_ref, wide_ref, out_ref, level_ref):
    bias = jnp.where(at_ref[0] == 1, 0.0, LOW).astype(f32)
    lane = iota((ROWS, DIM), 1)
    level_ref[...] = jnp.zeros_like(level_ref)

    def put(head, mean, level):
        out_ref[head] = mean.astype(bf16)
        level_ref[...] = jnp.where(lane == head, level, level_ref[...])

    attend_rows(query_ref, keys_ref, wide_ref, lambda s: s + bias, 4, put)
    level = level_ref[...]
    for part in range(3):
        cut = level.astype(bf16)
        out_ref[HEADS + part] = cut
        level = level - cut.astype(f32)


def attend_others(at, queries, keys, wide, name):
    elems = HEADS * ROWS * KEYS
    return pl.pallas_call(
        others_kernel,
        out_shape=jax.ShapeDtypeStruct((HEADS + 3, ROWS, DIM), bf16),
        in_specs=[scalars] + [whole] * 3,
        out_specs=whole,
        scratch_shapes=[pltpu.VMEM((ROWS, DIM), f32)],
        compiler_params=params(),
        name=name,
        cost_estimate=cost(elems * 768, 3e6, elems),
    )(at, queries, keys, wide)


def own_kernel(
    at_ref, query_ref, keys_ref, wide_ref, weight_ref, total_ref,
    mean_ref, level_ref, state_ref, gone_ref, fade_ref,
):
    first = at_ref[0] * ROWS
    visible = iota((ROWS, SLAB_KEYS), 1) - iota((ROWS, SLAB_KEYS), 0) <= first
    lane = iota((ROWS, DIM), 1)
    level_ref[...] = jnp.zeros_like(level_ref)

    def put(head, mean, level):
        mean_ref[head] = mean
        level_ref[...] = jnp.where(lane == head, level, level_ref[...])

    attend_rows(
        query_ref, keys_ref, wide_ref, lambda s: jnp.where(visible, s, LOW), 4, put
    )
    gone_ref[...] = fades(total_ref, fade_ref, at_ref[0])
    state_of(keys_ref, wide_ref, weight_ref, fade_ref, state_ref)


def attend_own(at, queries, keys, wide, weight, total):
    elems = HEADS * ROWS * KEYS
    return pl.pallas_call(
        own_kernel,
        out_shape=(
            jax.ShapeDtypeStruct((HEADS, ROWS, DIM), f32),
            jax.ShapeDtypeStruct((ROWS, DIM), f32),
            jax.ShapeDtypeStruct((HEADS * DIM, DIM), f32),
            jax.ShapeDtypeStruct((HEADS, DIM), f32),
        ),
        in_specs=[scalars] + [whole] * 5,
        out_specs=(whole,) * 4,
        scratch_shapes=[pltpu.VMEM((GROUP, HEADS, DIM), f32)],
        compiler_params=params(),
        name="attend_own",
        cost_estimate=cost(elems * 768, 4e6, elems),
    )(at, queries, keys, wide, weight, total)


def finish_kernel(
    at_ref, query_ref, decay_ref, inner_ref, mean_ref, level_ref, state_in, gone_ref, *refs
):
    means, states = refs[:3], refs[3:6]
    out_ref, sum_ref = refs[6:]
    me = at_ref[0]
    totals = [joined(s[HEADS * DIM:, :]) for s in states]
    gone = gone_ref[...]
    sum_ref[...] = state_in[...]
    for k in range(3):
        between = gone
        for j in range(3):
            inside = jnp.logical_and(at_ref[1 + j] > at_ref[1 + k], at_ref[1 + j] < me)
            between = between + jnp.where(inside, totals[j], 0.0)
        fade = jnp.where(at_ref[1 + k] < me, jnp.exp(-between), 0.0)
        for head in range(HEADS):
            span = slice(head * DIM, (head + 1) * DIM)
            sum_ref[span, :] += states[k][span, :].astype(f32) * fade[head:head + 1, :]
    levels = [level_ref[...]] + [
        m[HEADS].astype(f32) + m[HEADS + 1].astype(f32) + m[HEADS + 2].astype(f32) for m in means
    ]
    top = functools.reduce(jnp.maximum, levels)
    shares = [jnp.exp2(v - top) for v in levels]
    total = shares[0] + shares[1] + shares[2] + shares[3]
    shares = [s / total for s in shares]
    row, col = iota((ROWS, ROWS), 0), iota((ROWS, ROWS), 1)
    upto_rows = dot_nt((row >= col).astype(f32), decay_ref[...], exact)
    reach = jnp.exp(-upto_rows) * SCALE
    for head in range(HEADS):
        span = slice(head * DIM, (head + 1) * DIM)
        at = slice(head, head + 1)
        entering = dot(query_ref[:, span], sum_ref[span, :].astype(bf16))
        student = inner_ref[:, span] + entering * reach[:, at]
        teacher = mean_ref[head] * shares[0][:, at]
        for k in range(3):
            teacher = teacher + means[k][head].astype(f32) * shares[1 + k][:, at]
        out_ref[:, span] = (
            student.astype(bf16).astype(f32) - teacher.astype(bf16).astype(f32)
        ).astype(bf16)


def finish(at, queries, decay, inner, own, means, states):
    return pl.pallas_call(
        finish_kernel,
        out_shape=jax.ShapeDtypeStruct((ROWS, HEADS * DIM), bf16),
        in_specs=[scalars] + [whole] * 13,
        out_specs=whole,
        scratch_shapes=[pltpu.VMEM((HEADS * DIM, DIM), f32)],
        compiler_params=params(),
        name="finish",
        cost_estimate=cost(5e7, 4e6, 1e5),
    )(at, queries, decay, inner, *own, *means, *states)


def project_kernel(at_ref, *refs):
    rows, weights = refs[:4], refs[4:9]
    sent_ref, kept_ref, stack_ref = refs[9:]
    for r in range(4):
        stack_ref[r * ROWS:(r + 1) * ROWS, :] = rows[r][...]
    for w in range(4):
        for z in range(2):
            weight = weights[w][z] if w < 3 else weights[3 + z][0]
            result = dot(stack_ref[...], weight).astype(bf16)
            slot = at_ref[8 + w] * 2 + z

            @pl.when(at_ref[4 + w] == 0)
            def _(result=result, slot=slot):
                for r in range(4):
                    sent_ref[at_ref[r], slot] = result[r * ROWS:(r + 1) * ROWS]

            @pl.when(at_ref[4 + w] == 1)
            def _(result=result, slot=slot):
                for r in range(4):
                    kept_ref[at_ref[r], slot] = result[r * ROWS:(r + 1) * ROWS]


def project(at, rows, weights):
    depth, width = weights[0].shape[1:]
    out = jax.ShapeDtypeStruct((4, 4, ROWS, width), bf16)
    return pl.pallas_call(
        project_kernel,
        out_shape=(out, out),
        in_specs=[scalars] + [whole] * 9,
        out_specs=(whole, whole),
        scratch_shapes=[pltpu.VMEM((4 * ROWS, depth), bf16)],
        compiler_params=params(),
        name="project",
        cost_estimate=cost(2 * 8 * 4 * ROWS * depth * width, 8e6),
    )(at, *rows, *weights)


Y = ("yh", "yl")
SEQ = ("x", "yh", "yl", "zh")
TP = ("zl", "c")


def moved(value, axis, by, count):
    return lax.ppermute(value, axis, [(i, (i + by) % count) for i in range(count)])


def shards(
    queries,
    cache_keys,
    prefix_values,
    slab_key_rows,
    slab_value_rows,
    student_log_decay,
    student_step,
    student_skip_weight,
    out_weight,
):
    x, yh, yl, zh = (lax.axis_index(a) for a in SEQ)
    zl, core = (lax.axis_index(a) for a in TP)
    y = yh * 2 + yl
    steps = (0, -1, 1, -2)

    def numbers(*values):
        return jnp.stack([jnp.asarray(v).astype(jnp.int32) for v in values])

    def around(value, axis):
        return [moved(value, axis, by, 4) for by in (1, 3, 2)]

    skip = student_skip_weight.reshape(1, HEADS)
    own, decay, step = pack(
        slab_key_rows, slab_value_rows, cache_keys, prefix_values, student_log_decay, student_step
    )
    other = moved(own, "zh", 1, 2)
    inner = inner_block(queries, own, decay, step, skip)
    query_near = around(queries, "x")

    other, inner, weight_mine = lax.optimization_barrier((other, inner, out_weight))
    pair = jnp.concatenate(
        [jnp.where(zh == 0, own, other), jnp.where(zh == 0, other, own)], 0
    )
    near = around(pair, Y)
    weight_other = moved(weight_mine, "zh", 1, 2)

    near, weight_mine, weight_other = lax.optimization_barrier((near, weight_mine, weight_other))
    weight_pair = jnp.stack(
        [
            jnp.where(zh == 0, weight_mine, weight_other),
            jnp.where(zh == 0, weight_other, weight_mine),
        ]
    )
    weight_up, weight_down = moved(weight_pair, Y, 1, 4), moved(weight_pair, Y, 3, 4)

    keys, wide, state, weight, total = collect(
        numbers(*((y + d) % 4 for d in steps)), [pair] + near
    )
    states = around(state, "x")
    means = []
    for query, d, back in zip(query_near, steps[1:], (3, 1, 2)):
        place = (x + d) % 4
        mean = attend_others(numbers(place > x), query, keys, wide, "attend")
        means.append(moved(mean, "x", back, 4))
    weights = [
        weight_pair,
        weight_up,
        weight_down,
        moved(weight_up[:1], Y, 1, 4),
        moved(weight_down[1:], Y, 3, 4),
    ]
    mine = attend_own(numbers(y * 2 + zh), queries, keys, wide, weight, total)
    gap = finish(
        numbers(x, *((x + d) % 4 for d in steps[1:])), queries, decay, inner, mine, means, states
    )

    gaps = [gap] + around(gap, "x")
    column_places = [(y + d) % 4 for d in steps]
    at = [(x + d - zl) % 4 for d in steps]
    at += [jnp.where(p // 2 == core, 1, 0) for p in column_places]
    at += [p % 2 for p in column_places]
    sent, kept = project(numbers(*at), gaps, weights)
    from_core = moved(sent, "c", 1, 2)
    sums = kept.astype(f32) + from_core.astype(f32)
    pieces = [moved(sums[s].astype(bf16), "zl", s, 4) for s in (1, 2, 3)]
    summed = sums[0] + pieces[0].astype(f32) + pieces[1].astype(f32) + pieces[2].astype(f32)
    turned = lax.ppermute(
        summed.astype(bf16),
        ("zl", "x"),
        [(i * 4 + j, j * 4 + i) for i in range(4) for j in range(4)],
    )
    return jnp.transpose(turned, (1, 0, 2)).reshape(ROWS, HEADS * DIM)


def solution(mesh):
    devices = np.asarray(mesh.devices).reshape(4, 2, 4, 2, 2, 2)
    split = Mesh(devices, TP + SEQ)
    rows = P(SEQ, TP)
    heads = P(TP, SEQ)
    return jax.shard_map(
        shards,
        mesh=split,
        in_specs=(rows, rows, rows, rows, rows, heads, heads, P(TP), heads),
        out_specs=rows,
        check_vma=False,
    )
```

```python
import functools

import jax
import jax.numpy as jnp
import numpy as np
from jax import lax
from jax.experimental import pallas as pl
from jax.experimental.pallas import tpu as pltpu
from jax.sharding import Mesh
from jax.sharding import PartitionSpec as P

HEADS = 8
DIM = 128
ROWS = 128
CACHE = 256
META = 16
PACK = ROWS + META + CACHE
SCALE = DIM ** -0.5
SCALE2 = SCALE * 1.4426950408889634
LOW = -1e30
VMEM_LIMIT = 16 * 2**20
f32 = jnp.float32
bf16 = jnp.bfloat16
exact = lax.Precision.HIGHEST

whole = pl.BlockSpec(memory_space=pltpu.VMEM)
scalars = pl.BlockSpec(memory_space=pltpu.SMEM)


def full(shape):
    return pl.BlockSpec(shape, lambda i: (0,) * len(shape))


def params(limit=VMEM_LIMIT):
    return pltpu.CompilerParams(vmem_limit_bytes=limit)


def cost(flops, moved, exps=0):
    return pl.CostEstimate(flops=int(flops), bytes_accessed=int(moved), transcendentals=int(exps))


def dot_nt(a, b, precision=None):
    return lax.dot_general(
        a, b, (((1,), (1,)), ((), ())), preferred_element_type=f32, precision=precision
    )


def dot(a, b, precision=None):
    return jnp.dot(a, b, preferred_element_type=f32, precision=precision)


def iota(shape, axis):
    return lax.broadcasted_iota(jnp.int32, shape, axis)


def pack_kernel(
    key_ref, value_ref, cache_key_ref, cache_value_ref, decay_in, step_in,
    out_ref, decay_ref, step_ref, sems,
):
    copies = [
        pltpu.make_async_copy(decay_in, decay_ref, sems.at[0]),
        pltpu.make_async_copy(step_in, step_ref, sems.at[1]),
        pltpu.make_async_copy(key_ref, out_ref.at[0, 0:ROWS, 0:DIM], sems.at[2]),
        pltpu.make_async_copy(value_ref, out_ref.at[0, 0:ROWS, DIM:], sems.at[3]),
        pltpu.make_async_copy(cache_key_ref, out_ref.at[0, ROWS + META:, 0:DIM], sems.at[4]),
        pltpu.make_async_copy(cache_value_ref, out_ref.at[0, ROWS + META:, DIM:], sems.at[5]),
    ]
    for copy in copies:
        copy.start()
    copies[0].wait()
    copies[1].wait()
    decay = decay_ref[...]
    after = (iota((ROWS, ROWS), 0) > iota((ROWS, ROWS), 1)).astype(f32)
    to_end = dot(decay, after, exact)
    weight = jnp.exp(-to_end) * step_ref[...]
    total = jnp.broadcast_to(jnp.sum(decay, axis=1, keepdims=True), (HEADS, DIM))
    out_ref[0, ROWS:ROWS + META, 0:DIM] = two_parts(weight)
    out_ref[0, ROWS:ROWS + META, DIM:] = two_parts(total)
    for copy in copies[2:]:
        copy.wait()


def two_parts(value):
    high = value.astype(bf16)
    low = (value - high.astype(f32)).astype(bf16)
    return jnp.concatenate([high, low], 0)


def joined(parts):
    return parts[0:HEADS].astype(f32) + parts[HEADS:META].astype(f32)


def pack(keys, values, cache_keys, cache_values, decay, step):
    small = jax.ShapeDtypeStruct((HEADS, ROWS), f32)
    return pl.pallas_call(
        pack_kernel,
        out_shape=(jax.ShapeDtypeStruct((1, PACK, 2 * DIM), bf16), small, small),
        in_specs=[pl.BlockSpec(memory_space=pltpu.HBM)] * 6,
        out_specs=(whole,) * 3,
        scratch_shapes=[pltpu.SemaphoreType.DMA((6,))],
        compiler_params=params(60 * 2**20),
        name="pack",
        cost_estimate=cost(1e6, 5e5),
    )(keys, values, cache_keys, cache_values, decay, step)


def bundle_kernel(query_ref, weight_ref, out_ref, sems):
    depth, width = weight_ref.shape
    copies = [
        pltpu.make_async_copy(weight_ref, out_ref.at[0:depth, :], sems.at[HEADS // 2])
    ] + [
        pltpu.make_async_copy(
            query_ref.at[:, i * width:(i + 1) * width],
            out_ref.at[depth + i * ROWS:depth + (i + 1) * ROWS, :],
            sems.at[i],
        )
        for i in range(HEADS // 2)
    ]
    for copy in copies:
        copy.start()
    for copy in copies:
        copy.wait()


def bundle(queries, weight):
    hbm = pl.BlockSpec(memory_space=pltpu.HBM)
    return pl.pallas_call(
        bundle_kernel,
        out_shape=jax.ShapeDtypeStruct((weight.shape[0] + HEADS // 2 * ROWS, 2 * DIM), bf16),
        in_specs=[hbm] * 2,
        out_specs=whole,
        scratch_shapes=[pltpu.SemaphoreType.DMA((HEADS // 2 + 1,))],
        compiler_params=params(60 * 2**20),
        name="bundle",
        cost_estimate=cost(1e3, 2e6),
    )(queries, weight)


def inner_kernel(query_ref, block_ref, decay_ref, step_ref, skip_ref, inner_ref):
    keys = block_ref[0, 0:ROWS, 0:DIM]
    values = block_ref[0, 0:ROWS, DIM:]
    row, col = iota((ROWS, ROWS), 0), iota((ROWS, ROWS), 1)
    causal = row >= col
    decay = decay_ref[...]
    upto = dot(decay, (row <= col).astype(f32), exact)
    upto_rows = dot_nt((row >= col).astype(f32), decay, exact)
    value_f32 = values.astype(f32)
    for head in range(HEADS):
        span = slice(head * DIM, (head + 1) * DIM)
        scores = dot_nt(query_ref[:, span], keys)
        spread = upto_rows[:, head:head + 1] - upto[head:head + 1, :]
        fade = jnp.where(causal, jnp.exp(-jnp.where(causal, spread, 0.0)), 0.0)
        mixed = scores * (fade * (step_ref[head:head + 1, :] * SCALE))
        inner_ref[:, span] = dot(mixed.astype(bf16), values) + skip_ref[0, head] * value_f32


def inner_block(queries, own, decay, step, skip):
    return pl.pallas_call(
        inner_kernel,
        out_shape=jax.ShapeDtypeStruct((ROWS, HEADS * DIM), f32),
        in_specs=[whole] * 4 + [scalars],
        out_specs=whole,
        compiler_params=params(),
        name="inner",
        cost_estimate=cost(1e8, 1.5e6, 2e5),
    )(queries, own, decay, step, skip)


GROUP = 8
SLAB_KEYS = GROUP * ROWS
KEYS = GROUP * (ROWS + CACHE)


def fades(total_ref, fade_ref, last):
    def back(i, gone):
        place = GROUP - 1 - i
        live = place < last
        fade_ref[place] = jnp.where(live, jnp.exp(-gone), 0.0)
        return gone + jnp.where(live, total_ref[place], 0.0)

    return lax.fori_loop(0, GROUP, back, jnp.zeros((HEADS, DIM), f32))


def state_of(keys_ref, wide_ref, weight_ref, fade_ref, state_ref):
    state_ref[...] = jnp.zeros_like(state_ref)

    def step(i, carry):
        left = []
        for b in range(2):
            g = i * 2 + b
            weight = weight_ref[g] * fade_ref[g]
            turned = keys_ref[g].astype(f32)
            left.append(
                jnp.concatenate(
                    [(turned * weight[h:h + 1, :]).astype(bf16) for h in range(HEADS)], 0
                )
            )
        values = wide_ref[pl.ds(pl.multiple_of(i * 2 * ROWS, 2 * ROWS), 2 * ROWS), 0:DIM]
        state_ref[...] += dot(jnp.concatenate(left, 1), values)
        return carry

    lax.fori_loop(0, GROUP // 2, step, 0)


def collect_kernel(at_ref, *refs):
    pieces = refs[:GROUP]
    keys_ref, wide_ref, sent_ref, weight_ref, total_ref, fade_ref, state_ref = refs[GROUP:]
    wide_ref[:, DIM:] = jnp.ones((KEYS, DIM), bf16)
    for p, piece in enumerate(pieces):
        g = at_ref[p]
        slab = pl.ds(pl.multiple_of(g * ROWS, ROWS), ROWS)
        turned = piece[0, :, 0:DIM].astype(f32).T.astype(bf16)
        keys_ref[g] = turned[:, 0:ROWS]
        for half in range(2):
            at = ROWS + META + half * DIM
            keys_ref[GROUP + 2 * p + half] = turned[:, at:at + DIM]
        wide_ref[slab, 0:DIM] = piece[0, 0:ROWS, DIM:]
        wide_ref[SLAB_KEYS + p * CACHE:SLAB_KEYS + (p + 1) * CACHE, 0:DIM] = piece[
            0, ROWS + META:, DIM:
        ]
        weight_ref[g] = joined(piece[0, ROWS:ROWS + META, 0:DIM])
        total_ref[g] = joined(piece[0, ROWS:ROWS + META, DIM:])
    group_total = fades(total_ref, fade_ref, GROUP)
    state_of(keys_ref, wide_ref, weight_ref, fade_ref, state_ref)
    sent_ref[0:HEADS * DIM, :] = state_ref[...].astype(bf16)
    sent_ref[HEADS * DIM:, :] = two_parts(group_total)


def collect(at, pieces):
    table = jax.ShapeDtypeStruct((GROUP, HEADS, DIM), f32)
    return pl.pallas_call(
        collect_kernel,
        out_shape=(
            jax.ShapeDtypeStruct((KEYS // DIM, DIM, DIM), bf16),
            jax.ShapeDtypeStruct((KEYS, 2 * DIM), bf16),
            jax.ShapeDtypeStruct((HEADS * DIM + META, DIM), bf16),
            table,
            table,
        ),
        in_specs=[scalars] + [whole] * GROUP,
        out_specs=(whole,) * 5,
        scratch_shapes=[
            pltpu.VMEM((GROUP, HEADS, DIM), f32),
            pltpu.VMEM((HEADS * DIM, DIM), f32),
        ],
        compiler_params=params(),
        name="collect",
        cost_estimate=cost(3e8, 6e6, 1e5),
    )(at, *pieces)


def attend_rows(query_of, keys_ref, wide_ref, mask, put):
    for head in range(HEADS):
        query = query_of(head)
        for part in range(KEYS // SLAB_KEYS):
            tiles = [keys_ref[part * GROUP + t] for t in range(GROUP)]
            scores = dot(query, jnp.concatenate(tiles, 1))
            if part == 0:
                scores = mask(scores)
            highest = jnp.max(scores, axis=1, keepdims=True)
            top = highest if part == 0 else jnp.maximum(top, highest)
            weights = jnp.exp2((scores - top) * SCALE2).astype(bf16)
            added = dot(weights, wide_ref[part * SLAB_KEYS:(part + 1) * SLAB_KEYS, :])
            if part > 0:
                added = added + summed * jnp.exp2((before - top) * SCALE2)
            summed, before = added, top
        total = summed[:, DIM:]
        put(head, summed[:, :DIM] / total, top * SCALE2 + jnp.log2(total))


def others_kernel(at_ref, query_ref, keys_ref, wide_ref, out_ref, level_ref):
    bias = jnp.where(at_ref[0] == 1, 0.0, LOW).astype(f32)
    lane = iota((ROWS, DIM), 1)
    level_ref[...] = jnp.zeros_like(level_ref)

    def put(head, mean, level):
        out_ref[head] = mean.astype(bf16)
        level_ref[...] = jnp.where(lane == head, level, level_ref[...])

    def query_of(head):
        pair, side = head // 2, head % 2
        return query_ref[pair * ROWS:(pair + 1) * ROWS, side * DIM:(side + 1) * DIM]

    attend_rows(query_of, keys_ref, wide_ref, lambda s: s + bias, put)
    level = level_ref[...]
    spread = jnp.zeros_like(level)
    for part in range(3):
        cut = level.astype(bf16).astype(f32)
        spread = spread + (pltpu.roll(cut, part * HEADS, 1) if part else cut)
        level = level - cut
    out_ref[HEADS] = spread.astype(bf16)


def attend_others(at, bundled, keys, wide, name):
    elems = HEADS * ROWS * KEYS
    rows = HEADS // 2 * ROWS
    last = bundled.shape[0] // rows - 1
    return pl.pallas_call(
        others_kernel,
        grid=(1,),
        out_shape=jax.ShapeDtypeStruct((HEADS + 1, ROWS, DIM), bf16),
        in_specs=[scalars, pl.BlockSpec((rows, 2 * DIM), lambda i: (last, 0)), whole, whole],
        out_specs=whole,
        scratch_shapes=[pltpu.VMEM((ROWS, DIM), f32)],
        compiler_params=params(),
        name=name,
        cost_estimate=cost(elems * 768, 3e6, elems),
    )(at, bundled, keys, wide)


def own_kernel(
    at_ref, query_ref, keys_ref, wide_ref, weight_ref, total_ref,
    mean_ref, level_ref, state_ref, gone_ref, fade_ref,
):
    first = at_ref[0] * ROWS
    visible = iota((ROWS, SLAB_KEYS), 1) - iota((ROWS, SLAB_KEYS), 0) <= first
    lane = iota((ROWS, DIM), 1)
    level_ref[...] = jnp.zeros_like(level_ref)

    def put(head, mean, level):
        mean_ref[head] = mean
        level_ref[...] = jnp.where(lane == head, level, level_ref[...])

    attend_rows(
        lambda head: query_ref[:, head * DIM:(head + 1) * DIM],
        keys_ref,
        wide_ref,
        lambda s: jnp.where(visible, s, LOW),
        put,
    )
    gone_ref[...] = fades(total_ref, fade_ref, at_ref[0])
    state_of(keys_ref, wide_ref, weight_ref, fade_ref, state_ref)


def attend_own(at, queries, keys, wide, weight, total):
    elems = HEADS * ROWS * KEYS
    return pl.pallas_call(
        own_kernel,
        out_shape=(
            jax.ShapeDtypeStruct((HEADS, ROWS, DIM), f32),
            jax.ShapeDtypeStruct((ROWS, DIM), f32),
            jax.ShapeDtypeStruct((HEADS * DIM, DIM), f32),
            jax.ShapeDtypeStruct((HEADS, DIM), f32),
        ),
        in_specs=[scalars] + [whole] * 5,
        out_specs=(whole,) * 4,
        scratch_shapes=[pltpu.VMEM((GROUP, HEADS, DIM), f32)],
        compiler_params=params(),
        name="attend_own",
        cost_estimate=cost(elems * 768, 4e6, elems),
    )(at, queries, keys, wide, weight, total)


def finish_kernel(
    at_ref, query_ref, decay_ref, inner_ref, mean_ref, level_ref, state_in, gone_ref, *refs
):
    means, states = refs[:3], refs[3:6]
    out_ref, sum_ref = refs[6:]
    me = at_ref[0]
    totals = [joined(s[HEADS * DIM:, :]) for s in states]
    gone = gone_ref[...]
    sum_ref[...] = state_in[...]
    for k in range(3):
        between = gone
        for j in range(3):
            inside = jnp.logical_and(at_ref[1 + j] > at_ref[1 + k], at_ref[1 + j] < me)
            between = between + jnp.where(inside, totals[j], 0.0)
        fade = jnp.where(at_ref[1 + k] < me, jnp.exp(-between), 0.0)
        for head in range(HEADS):
            span = slice(head * DIM, (head + 1) * DIM)
            sum_ref[span, :] += states[k][span, :].astype(f32) * fade[head:head + 1, :]
    levels = [level_ref[...]]
    for mean in means:
        spread = mean[HEADS].astype(f32)
        levels.append(
            spread
            + pltpu.roll(spread, DIM - HEADS, 1)
            + pltpu.roll(spread, DIM - 2 * HEADS, 1)
        )
    top = functools.reduce(jnp.maximum, levels)
    shares = [jnp.exp2(v - top) for v in levels]
    total = shares[0] + shares[1] + shares[2] + shares[3]
    shares = [s / total for s in shares]
    row, col = iota((ROWS, ROWS), 0), iota((ROWS, ROWS), 1)
    upto_rows = dot_nt((row >= col).astype(f32), decay_ref[...], exact)
    reach = jnp.exp(-upto_rows) * SCALE
    for head in range(HEADS):
        span = slice(head * DIM, (head + 1) * DIM)
        at = slice(head, head + 1)
        entering = dot(query_ref[:, span], sum_ref[span, :].astype(bf16))
        student = inner_ref[:, span] + entering * reach[:, at]
        teacher = mean_ref[head] * shares[0][:, at]
        for k in range(3):
            teacher = teacher + means[k][head].astype(f32) * shares[1 + k][:, at]
        out_ref[:, span] = (
            student.astype(bf16).astype(f32) - teacher.astype(bf16).astype(f32)
        ).astype(bf16)


def finish(at, queries, decay, inner, own, means, states):
    return pl.pallas_call(
        finish_kernel,
        out_shape=jax.ShapeDtypeStruct((ROWS, HEADS * DIM), bf16),
        in_specs=[scalars] + [whole] * 13,
        out_specs=whole,
        scratch_shapes=[pltpu.VMEM((HEADS * DIM, DIM), f32)],
        compiler_params=params(),
        name="finish",
        cost_estimate=cost(5e7, 4e6, 1e5),
    )(at, queries, decay, inner, *own, *means, *states)


def project_kernel(at_ref, *refs):
    rows, weights = refs[:4], refs[4:13]
    sent_ref, kept_ref, stack_ref, held_ref, sems = refs[13:]
    depth = held_ref.shape[1]
    half = depth // 2
    copies = []
    for i, weight in enumerate(weights):
        if i < 7:
            source, target = weight.at[0:depth, :], held_ref.at[i]
        else:
            source, target = weight, held_ref.at[7, (i - 7) * half:(i - 6) * half, :]
        copies.append(pltpu.make_async_copy(source, target, sems.at[i]))
        copies[-1].start()
    for r in range(4):
        at = pl.multiple_of(at_ref[4 + r] * ROWS, ROWS)
        stack_ref[pl.ds(at, ROWS), :] = rows[r][...]
    for i in range(8):
        copies[i].wait()
        if i == 7:
            copies[8].wait()
        result = dot(stack_ref[...], held_ref[i]).astype(bf16)
        place, high = at_ref[i % 4], at_ref[8 + i // 4]
        for low in range(2):
            sent_ref[place, high, low] = result[low * ROWS:(low + 1) * ROWS]
            kept_ref[place, high, low] = result[(2 + low) * ROWS:(3 + low) * ROWS]


def project(at, rows, weights):
    depth, width = weights[0].shape
    out = jax.ShapeDtypeStruct((4, 2, 2, ROWS, width), bf16)
    return pl.pallas_call(
        project_kernel,
        out_shape=(out, out),
        in_specs=[scalars] + [whole] * 4 + [pl.BlockSpec(memory_space=pl.ANY)] * 9,
        out_specs=(whole, whole),
        scratch_shapes=[
            pltpu.VMEM((4 * ROWS, depth), bf16),
            pltpu.VMEM((8, depth, width), bf16),
            pltpu.SemaphoreType.DMA((9,)),
        ],
        compiler_params=params(),
        name="project",
        cost_estimate=cost(2 * 8 * 4 * ROWS * depth * width, 8e6),
    )(at, *rows, *weights)


Y = ("yh", "yl")
SEQ = ("x", "yh", "yl", "zh")
TP = ("zl", "c")


def moved(value, axis, by, count):
    return lax.ppermute(value, axis, [(i, (i + by) % count) for i in range(count)])


def shards(
    queries,
    cache_keys,
    prefix_values,
    slab_key_rows,
    slab_value_rows,
    student_log_decay,
    student_step,
    student_skip_weight,
    out_weight,
):
    x, yh, yl, zh = (lax.axis_index(a) for a in SEQ)
    zl, core = (lax.axis_index(a) for a in TP)
    y = yh * 2 + yl
    steps = (0, -1, 1, -2)

    def numbers(*values):
        return jnp.stack([jnp.asarray(v).astype(jnp.int32) for v in values])

    def around(value, axis):
        return [moved(value, axis, by, 4) for by in (1, 3, 2)]

    skip = student_skip_weight.reshape(1, HEADS)
    own, decay, step = pack(
        slab_key_rows, slab_value_rows, cache_keys, prefix_values, student_log_decay, student_step
    )
    other = moved(own, "zh", 1, 2)
    own_near = around(own, Y)
    bundled = around(bundle(queries, out_weight), "x")
    inner = inner_block(queries, own, decay, step, skip)
    other, inner, weight_mine = lax.optimization_barrier((other, inner, out_weight))
    other_near = around(other, Y)
    weight_other = moved(weight_mine, "zh", 1, 2)
    places = [((y + d) % 4) * 2 + zh for d in steps] + [((y + d) % 4) * 2 + 1 - zh for d in steps]
    keys, wide, state, weight, total = collect(
        numbers(*places), [own] + own_near + [other] + other_near
    )
    states = [
        lax.ppermute(state, "x", [(i, i + by) for i in range(4 - by)]) for by in (1, 2, 3)
    ]
    half = out_weight.shape[0] // 2

    def answer(index):
        place = (x + steps[1 + index]) % 4
        return attend_others(numbers(place > x), bundled[index], keys, wide, "attend")

    means = [answer(0)]
    means[0], bundled[1], weight_other = lax.optimization_barrier(
        (means[0], bundled[1], weight_other)
    )
    other_up, other_down = moved(weight_other, "x", 1, 4), moved(weight_other, "x", 3, 4)
    means.append(answer(1))
    means[1], bundled[2] = lax.optimization_barrier((means[1], bundled[2]))
    means.append(answer(2))
    means[2], own_query, *states = lax.optimization_barrier((means[2], queries, *states))
    mine = attend_own(numbers(y * 2 + zh), own_query, keys, wide, weight, total)
    means = [moved(mean, "x", back, 4) for mean, back in zip(means, (3, 1, 2))]
    mine, other_up, other_down = lax.optimization_barrier((mine, other_up, other_down))
    weights = [out_weight] + bundled + [
        weight_other,
        other_up,
        other_down,
        moved(other_up[:half], "x", 1, 4),
        moved(other_down[half:], "x", 3, 4),
    ]
    gap = finish(numbers(x, x - 1, x - 2, x - 3), queries, decay, inner, mine, means, states)

    gaps = [gap] + around(gap, Y)
    at = [(x + d - zl) % 4 for d in steps]
    row_places = [(y + d) % 4 for d in steps]
    at += [jnp.where(p // 2 == core, 2, 0) + p % 2 for p in row_places]
    at += [zh, 1 - zh]
    sent, kept = project(numbers(*at), gaps, weights)
    from_core = moved(sent, "c", 1, 2)
    sums = kept.astype(f32) + from_core.astype(f32)
    pieces = [moved(sums[s].astype(bf16), "zl", s, 4) for s in (1, 2, 3)]
    summed = sums[0] + pieces[0].astype(f32) + pieces[1].astype(f32) + pieces[2].astype(f32)
    summed = jnp.transpose(summed, (1, 2, 0, 3)).astype(bf16).reshape(2, ROWS, 2 * 256)
    same = lax.dynamic_index_in_dim(summed, yl, 0, False)
    cross = lax.dynamic_index_in_dim(summed, 1 - yl, 0, False)
    turn = ("c", "yh", "yl")
    pairs = [(h, w, k) for h in range(2) for w in range(2) for k in range(2)]
    same = lax.ppermute(
        same, turn, [(k * 4 + h * 2 + w, h * 4 + k * 2 + w) for h, w, k in pairs]
    )
    cross = lax.ppermute(
        cross, turn, [(k * 4 + h * 2 + w, h * 4 + k * 2 + 1 - w) for h, w, k in pairs]
    )
    return jnp.concatenate(
        [jnp.where(yl == 0, same, cross), jnp.where(yl == 0, cross, same)], 1
    )


def solution(mesh):
    devices = np.asarray(mesh.devices).reshape(4, 2, 4, 2, 2, 2)
    split = Mesh(devices, TP + SEQ)
    rows = P(SEQ, TP)
    heads = P(TP, SEQ)
    return jax.shard_map(
        shards,
        mesh=split,
        in_specs=(rows, rows, rows, rows, rows, heads, heads, P(TP), heads),
        out_specs=rows,
        check_vma=False,
    )
```

```python
import functools

import jax
import jax.numpy as jnp
import numpy as np
from jax import lax
from jax.experimental import pallas as pl
from jax.experimental.pallas import tpu as pltpu
from jax.sharding import Mesh
from jax.sharding import PartitionSpec as P

HEADS = 8
DIM = 128
ROWS = 128
CACHE = 256
META = 16
PACK = ROWS + META + CACHE
SCALE = DIM ** -0.5
SCALE2 = SCALE * 1.4426950408889634
LOW = -1e30
VMEM_LIMIT = 16 * 2**20
f32 = jnp.float32
bf16 = jnp.bfloat16
exact = lax.Precision.HIGHEST

whole = pl.BlockSpec(memory_space=pltpu.VMEM)
scalars = pl.BlockSpec(memory_space=pltpu.SMEM)


def full(shape):
    return pl.BlockSpec(shape, lambda i: (0,) * len(shape))


def params(limit=VMEM_LIMIT):
    return pltpu.CompilerParams(vmem_limit_bytes=limit)


def cost(flops, moved, exps=0):
    return pl.CostEstimate(flops=int(flops), bytes_accessed=int(moved), transcendentals=int(exps))


def dot_nt(a, b, precision=None):
    return lax.dot_general(
        a, b, (((1,), (1,)), ((), ())), preferred_element_type=f32, precision=precision
    )


def dot(a, b, precision=None):
    return jnp.dot(a, b, preferred_element_type=f32, precision=precision)


def iota(shape, axis):
    return lax.broadcasted_iota(jnp.int32, shape, axis)


def pack_kernel(
    key_ref, value_ref, cache_key_ref, cache_value_ref, decay_in, step_in,
    out_ref, decay_ref, step_ref, sems,
):
    copies = [
        pltpu.make_async_copy(decay_in, decay_ref, sems.at[0]),
        pltpu.make_async_copy(step_in, step_ref, sems.at[1]),
        pltpu.make_async_copy(key_ref, out_ref.at[0, 0:ROWS, 0:DIM], sems.at[2]),
        pltpu.make_async_copy(value_ref, out_ref.at[0, 0:ROWS, DIM:], sems.at[3]),
        pltpu.make_async_copy(cache_key_ref, out_ref.at[0, ROWS + META:, 0:DIM], sems.at[4]),
        pltpu.make_async_copy(cache_value_ref, out_ref.at[0, ROWS + META:, DIM:], sems.at[5]),
    ]
    for copy in copies:
        copy.start()
    copies[0].wait()
    copies[1].wait()
    decay = decay_ref[...]
    after = (iota((ROWS, ROWS), 0) > iota((ROWS, ROWS), 1)).astype(f32)
    to_end = dot(decay, after, exact)
    weight = jnp.exp(-to_end) * step_ref[...]
    total = jnp.broadcast_to(jnp.sum(decay, axis=1, keepdims=True), (HEADS, DIM))
    out_ref[0, ROWS:ROWS + META, 0:DIM] = two_parts(weight)
    out_ref[0, ROWS:ROWS + META, DIM:] = two_parts(total)
    for copy in copies[2:]:
        copy.wait()


def two_parts(value):
    high = value.astype(bf16)
    low = (value - high.astype(f32)).astype(bf16)
    return jnp.concatenate([high, low], 0)


def joined(parts):
    return parts[0:HEADS].astype(f32) + parts[HEADS:META].astype(f32)


def pack(keys, values, cache_keys, cache_values, decay, step):
    small = jax.ShapeDtypeStruct((HEADS, ROWS), f32)
    return pl.pallas_call(
        pack_kernel,
        out_shape=(jax.ShapeDtypeStruct((1, PACK, 2 * DIM), bf16), small, small),
        in_specs=[pl.BlockSpec(memory_space=pltpu.HBM)] * 6,
        out_specs=(whole,) * 3,
        scratch_shapes=[pltpu.SemaphoreType.DMA((6,))],
        compiler_params=params(60 * 2**20),
        name="pack",
        cost_estimate=cost(1e6, 5e5),
    )(keys, values, cache_keys, cache_values, decay, step)


def bundle_kernel(query_ref, weight_ref, out_ref, sems):
    depth, width = weight_ref.shape
    copies = [
        pltpu.make_async_copy(weight_ref, out_ref.at[0:depth, :], sems.at[HEADS // 2])
    ] + [
        pltpu.make_async_copy(
            query_ref.at[:, i * width:(i + 1) * width],
            out_ref.at[depth + i * ROWS:depth + (i + 1) * ROWS, :],
            sems.at[i],
        )
        for i in range(HEADS // 2)
    ]
    for copy in copies:
        copy.start()
    for copy in copies:
        copy.wait()


def bundle(queries, weight):
    hbm = pl.BlockSpec(memory_space=pltpu.HBM)
    return pl.pallas_call(
        bundle_kernel,
        out_shape=jax.ShapeDtypeStruct((weight.shape[0] + HEADS // 2 * ROWS, 2 * DIM), bf16),
        in_specs=[hbm] * 2,
        out_specs=whole,
        scratch_shapes=[pltpu.SemaphoreType.DMA((HEADS // 2 + 1,))],
        compiler_params=params(60 * 2**20),
        name="bundle",
        cost_estimate=cost(1e3, 2e6),
    )(queries, weight)


def inner_kernel(query_ref, block_ref, decay_ref, step_ref, skip_ref, inner_ref):
    keys = block_ref[0, 0:ROWS, 0:DIM]
    values = block_ref[0, 0:ROWS, DIM:]
    row, col = iota((ROWS, ROWS), 0), iota((ROWS, ROWS), 1)
    causal = row >= col
    decay = decay_ref[...]
    upto = dot(decay, (row <= col).astype(f32), exact)
    upto_rows = dot_nt((row >= col).astype(f32), decay, exact)
    value_f32 = values.astype(f32)
    for head in range(HEADS):
        span = slice(head * DIM, (head + 1) * DIM)
        scores = dot_nt(query_ref[:, span], keys)
        spread = upto_rows[:, head:head + 1] - upto[head:head + 1, :]
        fade = jnp.where(causal, jnp.exp(-jnp.where(causal, spread, 0.0)), 0.0)
        mixed = scores * (fade * (step_ref[head:head + 1, :] * SCALE))
        inner_ref[:, span] = dot(mixed.astype(bf16), values) + skip_ref[0, head] * value_f32


def inner_block(queries, own, decay, step, skip):
    return pl.pallas_call(
        inner_kernel,
        out_shape=jax.ShapeDtypeStruct((ROWS, HEADS * DIM), f32),
        in_specs=[whole] * 4 + [scalars],
        out_specs=whole,
        compiler_params=params(),
        name="inner",
        cost_estimate=cost(1e8, 1.5e6, 2e5),
    )(queries, own, decay, step, skip)


GROUP = 8
SLAB_KEYS = GROUP * ROWS
KEYS = GROUP * (ROWS + CACHE)


def fades(total_ref, fade_ref, last):
    def back(i, gone):
        place = GROUP - 1 - i
        live = place < last
        fade_ref[place] = jnp.where(live, jnp.exp(-gone), 0.0)
        return gone + jnp.where(live, total_ref[place], 0.0)

    return lax.fori_loop(0, GROUP, back, jnp.zeros((HEADS, DIM), f32))


def state_of(keys_ref, wide_ref, weight_ref, fade_ref, state_ref):
    state_ref[...] = jnp.zeros_like(state_ref)

    def step(i, carry):
        left = []
        for b in range(2):
            g = i * 2 + b
            weight = weight_ref[g] * fade_ref[g]
            turned = keys_ref[g].astype(f32)
            left.append(
                jnp.concatenate(
                    [(turned * weight[h:h + 1, :]).astype(bf16) for h in range(HEADS)], 0
                )
            )
        values = wide_ref[pl.ds(pl.multiple_of(i * 2 * ROWS, 2 * ROWS), 2 * ROWS), 0:DIM]
        state_ref[...] += dot(jnp.concatenate(left, 1), values)
        return carry

    lax.fori_loop(0, GROUP // 2, step, 0)


def collect_kernel(at_ref, *refs):
    pieces = refs[:GROUP]
    keys_ref, wide_ref, sent_ref, weight_ref, total_ref, fade_ref, state_ref = refs[GROUP:]
    wide_ref[:, DIM:] = jnp.ones((KEYS, DIM), bf16)
    for p, piece in enumerate(pieces):
        g = at_ref[p]
        slab = pl.ds(pl.multiple_of(g * ROWS, ROWS), ROWS)
        turned = piece[0, :, 0:DIM].astype(f32).T.astype(bf16)
        keys_ref[g] = turned[:, 0:ROWS]
        for half in range(2):
            at = ROWS + META + half * DIM
            keys_ref[GROUP + 2 * p + half] = turned[:, at:at + DIM]
        wide_ref[slab, 0:DIM] = piece[0, 0:ROWS, DIM:]
        wide_ref[SLAB_KEYS + p * CACHE:SLAB_KEYS + (p + 1) * CACHE, 0:DIM] = piece[
            0, ROWS + META:, DIM:
        ]
        weight_ref[g] = joined(piece[0, ROWS:ROWS + META, 0:DIM])
        total_ref[g] = joined(piece[0, ROWS:ROWS + META, DIM:])
    group_total = fades(total_ref, fade_ref, GROUP)
    state_of(keys_ref, wide_ref, weight_ref, fade_ref, state_ref)
    sent_ref[0:HEADS * DIM, :] = state_ref[...].astype(bf16)
    sent_ref[HEADS * DIM:, :] = two_parts(group_total)


def collect(at, pieces):
    table = jax.ShapeDtypeStruct((GROUP, HEADS, DIM), f32)
    return pl.pallas_call(
        collect_kernel,
        out_shape=(
            jax.ShapeDtypeStruct((KEYS // DIM, DIM, DIM), bf16),
            jax.ShapeDtypeStruct((KEYS, 2 * DIM), bf16),
            jax.ShapeDtypeStruct((HEADS * DIM + META, DIM), bf16),
            table,
            table,
        ),
        in_specs=[scalars] + [whole] * GROUP,
        out_specs=(whole,) * 5,
        scratch_shapes=[
            pltpu.VMEM((GROUP, HEADS, DIM), f32),
            pltpu.VMEM((HEADS * DIM, DIM), f32),
        ],
        compiler_params=params(),
        name="collect",
        cost_estimate=cost(3e8, 6e6, 1e5),
    )(at, *pieces)


def attend_rows(query_of, keys_ref, wide_ref, mask, put):
    for head in range(HEADS):
        query = query_of(head)
        for part in range(KEYS // SLAB_KEYS):
            tiles = [keys_ref[part * GROUP + t] for t in range(GROUP)]
            scores = dot(query, jnp.concatenate(tiles, 1))
            if part == 0:
                scores = mask(scores)
            highest = jnp.max(scores, axis=1, keepdims=True)
            top = highest if part == 0 else jnp.maximum(top, highest)
            weights = jnp.exp2((scores - top) * SCALE2).astype(bf16)
            added = dot(weights, wide_ref[part * SLAB_KEYS:(part + 1) * SLAB_KEYS, :])
            if part > 0:
                added = added + summed * jnp.exp2((before - top) * SCALE2)
            summed, before = added, top
        total = summed[:, DIM:]
        put(head, summed[:, :DIM] / total, top * SCALE2 + jnp.log2(total))


def others_kernel(at_ref, query_ref, keys_ref, wide_ref, out_ref, level_ref):
    bias = jnp.where(at_ref[0] == 1, 0.0, LOW).astype(f32)
    lane = iota((ROWS, DIM), 1)
    level_ref[...] = jnp.zeros_like(level_ref)

    def put(head, mean, level):
        out_ref[head] = mean.astype(bf16)
        level_ref[...] = jnp.where(lane == head, level, level_ref[...])

    def query_of(head):
        pair, side = head // 2, head % 2
        return query_ref[pair * ROWS:(pair + 1) * ROWS, side * DIM:(side + 1) * DIM]

    attend_rows(query_of, keys_ref, wide_ref, lambda s: s + bias, put)
    level = level_ref[...]
    spread = jnp.zeros_like(level)
    for part in range(3):
        cut = level.astype(bf16).astype(f32)
        spread = spread + (pltpu.roll(cut, part * HEADS, 1) if part else cut)
        level = level - cut
    out_ref[HEADS] = spread.astype(bf16)


def attend_others(at, bundled, keys, wide, name):
    elems = HEADS * ROWS * KEYS
    rows = HEADS // 2 * ROWS
    last = bundled.shape[0] // rows - 1
    return pl.pallas_call(
        others_kernel,
        grid=(1,),
        out_shape=jax.ShapeDtypeStruct((HEADS + 1, ROWS, DIM), bf16),
        in_specs=[scalars, pl.BlockSpec((rows, 2 * DIM), lambda i: (last, 0)), whole, whole],
        out_specs=whole,
        scratch_shapes=[pltpu.VMEM((ROWS, DIM), f32)],
        compiler_params=params(),
        name=name,
        cost_estimate=cost(elems * 768, 3e6, elems),
    )(at, bundled, keys, wide)


def own_kernel(
    at_ref, query_ref, keys_ref, wide_ref, weight_ref, total_ref,
    mean_ref, level_ref, state_ref, gone_ref, fade_ref,
):
    first = at_ref[0] * ROWS
    visible = iota((ROWS, SLAB_KEYS), 1) - iota((ROWS, SLAB_KEYS), 0) <= first
    lane = iota((ROWS, DIM), 1)
    level_ref[...] = jnp.zeros_like(level_ref)

    def put(head, mean, level):
        mean_ref[head] = mean
        level_ref[...] = jnp.where(lane == head, level, level_ref[...])

    attend_rows(
        lambda head: query_ref[:, head * DIM:(head + 1) * DIM],
        keys_ref,
        wide_ref,
        lambda s: jnp.where(visible, s, LOW),
        put,
    )
    gone_ref[...] = fades(total_ref, fade_ref, at_ref[0])
    state_of(keys_ref, wide_ref, weight_ref, fade_ref, state_ref)


def attend_own(at, queries, keys, wide, weight, total):
    elems = HEADS * ROWS * KEYS
    return pl.pallas_call(
        own_kernel,
        out_shape=(
            jax.ShapeDtypeStruct((HEADS, ROWS, DIM), f32),
            jax.ShapeDtypeStruct((ROWS, DIM), f32),
            jax.ShapeDtypeStruct((HEADS * DIM, DIM), f32),
            jax.ShapeDtypeStruct((HEADS, DIM), f32),
        ),
        in_specs=[scalars] + [whole] * 5,
        out_specs=(whole,) * 4,
        scratch_shapes=[pltpu.VMEM((GROUP, HEADS, DIM), f32)],
        compiler_params=params(),
        name="attend_own",
        cost_estimate=cost(elems * 768, 4e6, elems),
    )(at, queries, keys, wide, weight, total)


def finish_kernel(
    at_ref, query_ref, decay_ref, inner_ref, mean_ref, level_ref, state_in, gone_ref, *refs
):
    means, states = refs[:3], refs[3:6]
    out_ref, sum_ref = refs[6:]
    me = at_ref[0]
    totals = [joined(s[HEADS * DIM:, :]) for s in states]
    gone = gone_ref[...]
    sum_ref[...] = state_in[...]
    for k in range(3):
        between = gone
        for j in range(3):
            inside = jnp.logical_and(at_ref[1 + j] > at_ref[1 + k], at_ref[1 + j] < me)
            between = between + jnp.where(inside, totals[j], 0.0)
        fade = jnp.where(at_ref[1 + k] < me, jnp.exp(-between), 0.0)
        for head in range(HEADS):
            span = slice(head * DIM, (head + 1) * DIM)
            sum_ref[span, :] += states[k][span, :].astype(f32) * fade[head:head + 1, :]
    levels = [level_ref[...]]
    for mean in means:
        spread = mean[HEADS].astype(f32)
        levels.append(
            spread
            + pltpu.roll(spread, DIM - HEADS, 1)
            + pltpu.roll(spread, DIM - 2 * HEADS, 1)
        )
    top = functools.reduce(jnp.maximum, levels)
    shares = [jnp.exp2(v - top) for v in levels]
    total = shares[0] + shares[1] + shares[2] + shares[3]
    shares = [s / total for s in shares]
    row, col = iota((ROWS, ROWS), 0), iota((ROWS, ROWS), 1)
    upto_rows = dot_nt((row >= col).astype(f32), decay_ref[...], exact)
    reach = jnp.exp(-upto_rows) * SCALE
    for head in range(HEADS):
        span = slice(head * DIM, (head + 1) * DIM)
        at = slice(head, head + 1)
        entering = dot(query_ref[:, span], sum_ref[span, :].astype(bf16))
        student = inner_ref[:, span] + entering * reach[:, at]
        teacher = mean_ref[head] * shares[0][:, at]
        for k in range(3):
            teacher = teacher + means[k][head].astype(f32) * shares[1 + k][:, at]
        out_ref[:, span] = (
            student.astype(bf16).astype(f32) - teacher.astype(bf16).astype(f32)
        ).astype(bf16)


def finish(at, queries, decay, inner, own, means, states):
    return pl.pallas_call(
        finish_kernel,
        out_shape=jax.ShapeDtypeStruct((ROWS, HEADS * DIM), bf16),
        in_specs=[scalars] + [whole] * 13,
        out_specs=whole,
        scratch_shapes=[pltpu.VMEM((HEADS * DIM, DIM), f32)],
        compiler_params=params(),
        name="finish",
        cost_estimate=cost(5e7, 4e6, 1e5),
    )(at, queries, decay, inner, *own, *means, *states)


def project_kernel(at_ref, *refs):
    rows, weights = refs[:4], refs[4:13]
    sent_ref, kept_ref, stack_ref, held_ref, sems = refs[13:]
    depth = held_ref.shape[1]
    half = depth // 2
    copies = []
    for i, weight in enumerate(weights):
        if i < 7:
            source, target = weight.at[0:depth, :], held_ref.at[i]
        else:
            source, target = weight, held_ref.at[7, (i - 7) * half:(i - 6) * half, :]
        copies.append(pltpu.make_async_copy(source, target, sems.at[i]))
        copies[-1].start()
    for r in range(4):
        at = pl.multiple_of(at_ref[4 + r] * ROWS, ROWS)
        stack_ref[pl.ds(at, ROWS), :] = rows[r][...]
    for i in range(8):
        copies[i].wait()
        if i == 7:
            copies[8].wait()
        result = dot(stack_ref[...], held_ref[i]).astype(bf16)
        place, high = at_ref[i % 4], at_ref[8 + i // 4]
        for low in range(2):
            sent_ref[place, high, low] = result[low * ROWS:(low + 1) * ROWS]
            kept_ref[place, high, low] = result[(2 + low) * ROWS:(3 + low) * ROWS]


def project(at, rows, weights):
    depth, width = weights[0].shape
    out = jax.ShapeDtypeStruct((4, 2, 2, ROWS, width), bf16)
    return pl.pallas_call(
        project_kernel,
        out_shape=(out, out),
        in_specs=[scalars] + [whole] * 4 + [pl.BlockSpec(memory_space=pl.ANY)] * 9,
        out_specs=(whole, whole),
        scratch_shapes=[
            pltpu.VMEM((4 * ROWS, depth), bf16),
            pltpu.VMEM((8, depth, width), bf16),
            pltpu.SemaphoreType.DMA((9,)),
        ],
        compiler_params=params(),
        name="project",
        cost_estimate=cost(2 * 8 * 4 * ROWS * depth * width, 8e6),
    )(at, *rows, *weights)


Y = ("yh", "yl")
SEQ = ("x", "yh", "yl", "zh")
TP = ("zl", "c")


def moved(value, axis, by, count):
    return lax.ppermute(value, axis, [(i, (i + by) % count) for i in range(count)])


def shards(
    queries,
    cache_keys,
    prefix_values,
    slab_key_rows,
    slab_value_rows,
    student_log_decay,
    student_step,
    student_skip_weight,
    out_weight,
):
    x, yh, yl, zh = (lax.axis_index(a) for a in SEQ)
    zl, core = (lax.axis_index(a) for a in TP)
    y = yh * 2 + yl
    steps = (0, -1, 1, -2)

    def numbers(*values):
        return jnp.stack([jnp.asarray(v).astype(jnp.int32) for v in values])

    def around(value, axis):
        return [moved(value, axis, by, 4) for by in (1, 3, 2)]

    skip = student_skip_weight.reshape(1, HEADS)
    own, decay, step = pack(
        slab_key_rows, slab_value_rows, cache_keys, prefix_values, student_log_decay, student_step
    )
    other = moved(own, "zh", 1, 2)
    own_near = around(own, Y)
    own, bundle_query = lax.optimization_barrier((own, queries))
    bundled = around(bundle(bundle_query, out_weight), "x")
    inner = inner_block(queries, own, decay, step, skip)
    other, inner = lax.optimization_barrier((other, inner))
    other_near = around(other, Y)
    own_near[1], weight_mine = lax.optimization_barrier((own_near[1], out_weight))
    weight_other = moved(weight_mine, "zh", 1, 2)
    places = [((y + d) % 4) * 2 + zh for d in steps] + [((y + d) % 4) * 2 + 1 - zh for d in steps]
    keys, wide, state, weight, total = collect(
        numbers(*places), [own] + own_near + [other] + other_near
    )
    states = [
        lax.ppermute(state, "x", [(i, i + by) for i in range(4 - by)]) for by in (1, 2, 3)
    ]
    half = out_weight.shape[0] // 2

    def answer(index):
        place = (x + steps[1 + index]) % 4
        return attend_others(numbers(place > x), bundled[index], keys, wide, "attend")

    means = [answer(0)]
    means[0], bundled[1] = lax.optimization_barrier((means[0], bundled[1]))
    means.append(answer(1))
    means[1], bundled[2], weight_other = lax.optimization_barrier(
        (means[1], bundled[2], weight_other)
    )
    other_up, other_down = moved(weight_other, "x", 1, 4), moved(weight_other, "x", 3, 4)
    means.append(answer(2))
    means[2], own_query, *states = lax.optimization_barrier((means[2], queries, *states))
    mine = attend_own(numbers(y * 2 + zh), own_query, keys, wide, weight, total)
    means = [moved(mean, "x", back, 4) for mean, back in zip(means, (3, 1, 2))]
    mine, other_up, other_down = lax.optimization_barrier((mine, other_up, other_down))
    weights = [out_weight] + bundled + [
        weight_other,
        other_up,
        other_down,
        moved(other_up[:half], "x", 1, 4),
        moved(other_down[half:], "x", 3, 4),
    ]
    gap = finish(numbers(x, x - 1, x - 2, x - 3), queries, decay, inner, mine, means, states)

    gaps = [gap] + around(gap, Y)
    at = [(x + d - zl) % 4 for d in steps]
    row_places = [(y + d) % 4 for d in steps]
    at += [jnp.where(p // 2 == core, 2, 0) + p % 2 for p in row_places]
    at += [zh, 1 - zh]
    sent, kept = project(numbers(*at), gaps, weights)
    from_core = moved(sent, "c", 1, 2)
    sums = kept.astype(f32) + from_core.astype(f32)
    pieces = [moved(sums[s].astype(bf16), "zl", s, 4) for s in (1, 2, 3)]
    summed = sums[0] + pieces[0].astype(f32) + pieces[1].astype(f32) + pieces[2].astype(f32)
    summed = jnp.transpose(summed, (1, 2, 0, 3)).astype(bf16).reshape(2, ROWS, 2 * 256)
    same = lax.dynamic_index_in_dim(summed, yl, 0, False)
    cross = lax.dynamic_index_in_dim(summed, 1 - yl, 0, False)
    turn = ("c", "yh", "yl")
    pairs = [(h, w, k) for h in range(2) for w in range(2) for k in range(2)]
    same = lax.ppermute(
        same, turn, [(k * 4 + h * 2 + w, h * 4 + k * 2 + w) for h, w, k in pairs]
    )
    cross = lax.ppermute(
        cross, turn, [(k * 4 + h * 2 + w, h * 4 + k * 2 + 1 - w) for h, w, k in pairs]
    )
    return jnp.concatenate(
        [jnp.where(yl == 0, same, cross), jnp.where(yl == 0, cross, same)], 1
    )


def solution(mesh):
    devices = np.asarray(mesh.devices).reshape(4, 2, 4, 2, 2, 2)
    split = Mesh(devices, TP + SEQ)
    rows = P(SEQ, TP)
    heads = P(TP, SEQ)
    return jax.shard_map(
        shards,
        mesh=split,
        in_specs=(rows, rows, rows, rows, rows, heads, heads, P(TP), heads),
        out_specs=rows,
        check_vma=False,
    )
```

```python
import functools

import jax
import jax.numpy as jnp
import numpy as np
from jax import lax
from jax.experimental import pallas as pl
from jax.experimental.pallas import tpu as pltpu
from jax.sharding import Mesh
from jax.sharding import PartitionSpec as P

HEADS = 8
DIM = 128
ROWS = 128
CACHE = 256
META = 16
PACK = ROWS + META + CACHE
SCALE = DIM ** -0.5
SCALE2 = SCALE * 1.4426950408889634
LOW = -1e30
VMEM_LIMIT = 16 * 2**20
f32 = jnp.float32
bf16 = jnp.bfloat16
exact = lax.Precision.HIGHEST

whole = pl.BlockSpec(memory_space=pltpu.VMEM)
scalars = pl.BlockSpec(memory_space=pltpu.SMEM)


def full(shape):
    return pl.BlockSpec(shape, lambda i: (0,) * len(shape))


def params(limit=VMEM_LIMIT):
    return pltpu.CompilerParams(vmem_limit_bytes=limit)


def cost(flops, moved, exps=0):
    return pl.CostEstimate(flops=int(flops), bytes_accessed=int(moved), transcendentals=int(exps))


def dot_nt(a, b, precision=None):
    return lax.dot_general(
        a, b, (((1,), (1,)), ((), ())), preferred_element_type=f32, precision=precision
    )


def dot(a, b, precision=None):
    return jnp.dot(a, b, preferred_element_type=f32, precision=precision)


def iota(shape, axis):
    return lax.broadcasted_iota(jnp.int32, shape, axis)


def pack_kernel(
    key_ref, value_ref, cache_key_ref, cache_value_ref, decay_in, step_in,
    out_ref, decay_ref, step_ref, sems,
):
    copies = [
        pltpu.make_async_copy(decay_in, decay_ref, sems.at[0]),
        pltpu.make_async_copy(step_in, step_ref, sems.at[1]),
        pltpu.make_async_copy(key_ref, out_ref.at[0, 0:ROWS, 0:DIM], sems.at[2]),
        pltpu.make_async_copy(value_ref, out_ref.at[0, 0:ROWS, DIM:], sems.at[3]),
        pltpu.make_async_copy(cache_key_ref, out_ref.at[0, ROWS + META:, 0:DIM], sems.at[4]),
        pltpu.make_async_copy(cache_value_ref, out_ref.at[0, ROWS + META:, DIM:], sems.at[5]),
    ]
    for copy in copies:
        copy.start()
    copies[0].wait()
    copies[1].wait()
    decay = decay_ref[...]
    after = (iota((ROWS, ROWS), 0) > iota((ROWS, ROWS), 1)).astype(f32)
    to_end = dot(decay, after, exact)
    weight = jnp.exp(-to_end) * step_ref[...]
    total = jnp.broadcast_to(jnp.sum(decay, axis=1, keepdims=True), (HEADS, DIM))
    out_ref[0, ROWS:ROWS + META, 0:DIM] = two_parts(weight)
    out_ref[0, ROWS:ROWS + META, DIM:] = two_parts(total)
    for copy in copies[2:]:
        copy.wait()


def two_parts(value):
    high = value.astype(bf16)
    low = (value - high.astype(f32)).astype(bf16)
    return jnp.concatenate([high, low], 0)


def joined(parts):
    return parts[0:HEADS].astype(f32) + parts[HEADS:META].astype(f32)


def pack(keys, values, cache_keys, cache_values, decay, step):
    small = jax.ShapeDtypeStruct((HEADS, ROWS), f32)
    return pl.pallas_call(
        pack_kernel,
        out_shape=(jax.ShapeDtypeStruct((1, PACK, 2 * DIM), bf16), small, small),
        in_specs=[pl.BlockSpec(memory_space=pltpu.HBM)] * 6,
        out_specs=(whole,) * 3,
        scratch_shapes=[pltpu.SemaphoreType.DMA((6,))],
        compiler_params=params(60 * 2**20),
        name="pack",
        cost_estimate=cost(1e6, 5e5),
    )(keys, values, cache_keys, cache_values, decay, step)


def bundle_kernel(query_ref, weight_ref, out_ref, sems):
    depth, width = weight_ref.shape
    copies = [
        pltpu.make_async_copy(weight_ref, out_ref.at[0:depth, :], sems.at[HEADS // 2])
    ] + [
        pltpu.make_async_copy(
            query_ref.at[:, i * width:(i + 1) * width],
            out_ref.at[depth + i * ROWS:depth + (i + 1) * ROWS, :],
            sems.at[i],
        )
        for i in range(HEADS // 2)
    ]
    for copy in copies:
        copy.start()
    for copy in copies:
        copy.wait()


def bundle(queries, weight):
    hbm = pl.BlockSpec(memory_space=pltpu.HBM)
    return pl.pallas_call(
        bundle_kernel,
        out_shape=jax.ShapeDtypeStruct((weight.shape[0] + HEADS // 2 * ROWS, 2 * DIM), bf16),
        in_specs=[hbm] * 2,
        out_specs=whole,
        scratch_shapes=[pltpu.SemaphoreType.DMA((HEADS // 2 + 1,))],
        compiler_params=params(60 * 2**20),
        name="bundle",
        cost_estimate=cost(1e3, 2e6),
    )(queries, weight)


def inner_kernel(query_ref, block_ref, decay_ref, step_ref, skip_ref, inner_ref):
    keys = block_ref[0, 0:ROWS, 0:DIM]
    values = block_ref[0, 0:ROWS, DIM:]
    row, col = iota((ROWS, ROWS), 0), iota((ROWS, ROWS), 1)
    causal = row >= col
    decay = decay_ref[...]
    upto = dot(decay, (row <= col).astype(f32), exact)
    upto_rows = dot_nt((row >= col).astype(f32), decay, exact)
    value_f32 = values.astype(f32)
    for head in range(HEADS):
        span = slice(head * DIM, (head + 1) * DIM)
        scores = dot_nt(query_ref[:, span], keys)
        spread = upto_rows[:, head:head + 1] - upto[head:head + 1, :]
        fade = jnp.where(causal, jnp.exp(-jnp.where(causal, spread, 0.0)), 0.0)
        mixed = scores * (fade * (step_ref[head:head + 1, :] * SCALE))
        inner_ref[:, span] = dot(mixed.astype(bf16), values) + skip_ref[0, head] * value_f32


def inner_block(queries, own, decay, step, skip):
    return pl.pallas_call(
        inner_kernel,
        grid=(1,),
        out_shape=jax.ShapeDtypeStruct((ROWS, HEADS * DIM), f32),
        in_specs=[
            pl.BlockSpec((ROWS, HEADS * DIM), lambda i: (0, 0)),
            pl.BlockSpec((1, PACK, 2 * DIM), lambda i: (0, 0, 0)),
            pl.BlockSpec((HEADS, ROWS), lambda i: (0, 0)),
            pl.BlockSpec((HEADS, ROWS), lambda i: (0, 0)),
            scalars,
        ],
        out_specs=pl.BlockSpec((ROWS, HEADS * DIM), lambda i: (0, 0)),
        compiler_params=params(60 * 2**20),
        name="inner",
        cost_estimate=cost(1e8, 1.5e6, 2e5),
    )(queries, own, decay, step, skip)


GROUP = 8
SLAB_KEYS = GROUP * ROWS
KEYS = GROUP * (ROWS + CACHE)


def fades(total_ref, fade_ref, last):
    def back(i, gone):
        place = GROUP - 1 - i
        live = place < last
        fade_ref[place] = jnp.where(live, jnp.exp(-gone), 0.0)
        return gone + jnp.where(live, total_ref[place], 0.0)

    return lax.fori_loop(0, GROUP, back, jnp.zeros((HEADS, DIM), f32))


def state_of(keys_ref, wide_ref, weight_ref, fade_ref, state_ref):
    state_ref[...] = jnp.zeros_like(state_ref)

    def step(i, carry):
        left = []
        for b in range(2):
            g = i * 2 + b
            weight = weight_ref[g] * fade_ref[g]
            turned = keys_ref[g].astype(f32)
            left.append(
                jnp.concatenate(
                    [(turned * weight[h:h + 1, :]).astype(bf16) for h in range(HEADS)], 0
                )
            )
        values = wide_ref[pl.ds(pl.multiple_of(i * 2 * ROWS, 2 * ROWS), 2 * ROWS), 0:DIM]
        state_ref[...] += dot(jnp.concatenate(left, 1), values)
        return carry

    lax.fori_loop(0, GROUP // 2, step, 0)


def collect_kernel(at_ref, *refs):
    pieces = refs[:GROUP]
    keys_ref, wide_ref, sent_ref, weight_ref, total_ref, fade_ref, state_ref = refs[GROUP:]
    wide_ref[:, DIM:] = jnp.ones((KEYS, DIM), bf16)
    for p, piece in enumerate(pieces):
        g = at_ref[p]
        slab = pl.ds(pl.multiple_of(g * ROWS, ROWS), ROWS)
        turned = piece[0, :, 0:DIM].astype(f32).T.astype(bf16)
        keys_ref[g] = turned[:, 0:ROWS]
        for half in range(2):
            at = ROWS + META + half * DIM
            keys_ref[GROUP + 2 * p + half] = turned[:, at:at + DIM]
        wide_ref[slab, 0:DIM] = piece[0, 0:ROWS, DIM:]
        wide_ref[SLAB_KEYS + p * CACHE:SLAB_KEYS + (p + 1) * CACHE, 0:DIM] = piece[
            0, ROWS + META:, DIM:
        ]
        weight_ref[g] = joined(piece[0, ROWS:ROWS + META, 0:DIM])
        total_ref[g] = joined(piece[0, ROWS:ROWS + META, DIM:])
    group_total = fades(total_ref, fade_ref, GROUP)
    state_of(keys_ref, wide_ref, weight_ref, fade_ref, state_ref)
    sent_ref[0:HEADS * DIM, :] = state_ref[...].astype(bf16)
    sent_ref[HEADS * DIM:, :] = two_parts(group_total)


def collect(at, pieces):
    table = jax.ShapeDtypeStruct((GROUP, HEADS, DIM), f32)
    return pl.pallas_call(
        collect_kernel,
        out_shape=(
            jax.ShapeDtypeStruct((KEYS // DIM, DIM, DIM), bf16),
            jax.ShapeDtypeStruct((KEYS, 2 * DIM), bf16),
            jax.ShapeDtypeStruct((HEADS * DIM + META, DIM), bf16),
            table,
            table,
        ),
        in_specs=[scalars] + [whole] * GROUP,
        out_specs=(whole,) * 5,
        scratch_shapes=[
            pltpu.VMEM((GROUP, HEADS, DIM), f32),
            pltpu.VMEM((HEADS * DIM, DIM), f32),
        ],
        compiler_params=params(),
        name="collect",
        cost_estimate=cost(3e8, 6e6, 1e5),
    )(at, *pieces)


def attend_rows(query_of, keys_ref, wide_ref, mask, put):
    for head in range(HEADS):
        query = query_of(head)
        for part in range(KEYS // SLAB_KEYS):
            tiles = [keys_ref[part * GROUP + t] for t in range(GROUP)]
            scores = dot(query, jnp.concatenate(tiles, 1))
            if part == 0:
                scores = mask(scores)
            highest = jnp.max(scores, axis=1, keepdims=True)
            top = highest if part == 0 else jnp.maximum(top, highest)
            weights = jnp.exp2((scores - top) * SCALE2).astype(bf16)
            added = dot(weights, wide_ref[part * SLAB_KEYS:(part + 1) * SLAB_KEYS, :])
            if part > 0:
                added = added + summed * jnp.exp2((before - top) * SCALE2)
            summed, before = added, top
        total = summed[:, DIM:]
        put(head, summed[:, :DIM] / total, top * SCALE2 + jnp.log2(total))


def others_kernel(at_ref, query_ref, keys_ref, wide_ref, out_ref, level_ref):
    bias = jnp.where(at_ref[0] == 1, 0.0, LOW).astype(f32)
    lane = iota((ROWS, DIM), 1)
    level_ref[...] = jnp.zeros_like(level_ref)

    def put(head, mean, level):
        out_ref[head] = mean.astype(bf16)
        level_ref[...] = jnp.where(lane == head, level, level_ref[...])

    def query_of(head):
        pair, side = head // 2, head % 2
        return query_ref[pair * ROWS:(pair + 1) * ROWS, side * DIM:(side + 1) * DIM]

    attend_rows(query_of, keys_ref, wide_ref, lambda s: s + bias, put)
    level = level_ref[...]
    spread = jnp.zeros_like(level)
    for part in range(3):
        cut = level.astype(bf16).astype(f32)
        spread = spread + (pltpu.roll(cut, part * HEADS, 1) if part else cut)
        level = level - cut
    out_ref[HEADS] = spread.astype(bf16)


def attend_others(at, bundled, keys, wide, name):
    elems = HEADS * ROWS * KEYS
    rows = HEADS // 2 * ROWS
    last = bundled.shape[0] // rows - 1
    return pl.pallas_call(
        others_kernel,
        grid=(1,),
        out_shape=jax.ShapeDtypeStruct((HEADS + 1, ROWS, DIM), bf16),
        in_specs=[scalars, pl.BlockSpec((rows, 2 * DIM), lambda i: (last, 0)), whole, whole],
        out_specs=whole,
        scratch_shapes=[pltpu.VMEM((ROWS, DIM), f32)],
        compiler_params=params(),
        name=name,
        cost_estimate=cost(elems * 768, 3e6, elems),
    )(at, bundled, keys, wide)


def own_kernel(
    at_ref, query_ref, keys_ref, wide_ref, weight_ref, total_ref,
    mean_ref, level_ref, state_ref, gone_ref, fade_ref,
):
    first = at_ref[0] * ROWS
    visible = iota((ROWS, SLAB_KEYS), 1) - iota((ROWS, SLAB_KEYS), 0) <= first
    lane = iota((ROWS, DIM), 1)
    level_ref[...] = jnp.zeros_like(level_ref)

    def put(head, mean, level):
        mean_ref[head] = mean
        level_ref[...] = jnp.where(lane == head, level, level_ref[...])

    attend_rows(
        lambda head: query_ref[:, head * DIM:(head + 1) * DIM],
        keys_ref,
        wide_ref,
        lambda s: jnp.where(visible, s, LOW),
        put,
    )
    gone_ref[...] = fades(total_ref, fade_ref, at_ref[0])
    state_of(keys_ref, wide_ref, weight_ref, fade_ref, state_ref)


def attend_own(at, queries, keys, wide, weight, total):
    elems = HEADS * ROWS * KEYS
    return pl.pallas_call(
        own_kernel,
        out_shape=(
            jax.ShapeDtypeStruct((HEADS, ROWS, DIM), f32),
            jax.ShapeDtypeStruct((ROWS, DIM), f32),
            jax.ShapeDtypeStruct((HEADS * DIM, DIM), f32),
            jax.ShapeDtypeStruct((HEADS, DIM), f32),
        ),
        in_specs=[scalars] + [whole] * 5,
        out_specs=(whole,) * 4,
        scratch_shapes=[pltpu.VMEM((GROUP, HEADS, DIM), f32)],
        compiler_params=params(),
        name="attend_own",
        cost_estimate=cost(elems * 768, 4e6, elems),
    )(at, queries, keys, wide, weight, total)


def finish_kernel(
    at_ref, query_ref, decay_ref, inner_ref, mean_ref, level_ref, state_in, gone_ref, *refs
):
    means, states = refs[:3], refs[3:6]
    out_ref, sum_ref = refs[6:]
    me = at_ref[0]
    totals = [joined(s[HEADS * DIM:, :]) for s in states]
    gone = gone_ref[...]
    sum_ref[...] = state_in[...]
    for k in range(3):
        between = gone
        for j in range(3):
            inside = jnp.logical_and(at_ref[1 + j] > at_ref[1 + k], at_ref[1 + j] < me)
            between = between + jnp.where(inside, totals[j], 0.0)
        fade = jnp.where(at_ref[1 + k] < me, jnp.exp(-between), 0.0)
        for head in range(HEADS):
            span = slice(head * DIM, (head + 1) * DIM)
            sum_ref[span, :] += states[k][span, :].astype(f32) * fade[head:head + 1, :]
    levels = [level_ref[...]]
    for mean in means:
        spread = mean[HEADS].astype(f32)
        levels.append(
            spread
            + pltpu.roll(spread, DIM - HEADS, 1)
            + pltpu.roll(spread, DIM - 2 * HEADS, 1)
        )
    top = functools.reduce(jnp.maximum, levels)
    shares = [jnp.exp2(v - top) for v in levels]
    total = shares[0] + shares[1] + shares[2] + shares[3]
    shares = [s / total for s in shares]
    row, col = iota((ROWS, ROWS), 0), iota((ROWS, ROWS), 1)
    upto_rows = dot_nt((row >= col).astype(f32), decay_ref[...], exact)
    reach = jnp.exp(-upto_rows) * SCALE
    for head in range(HEADS):
        span = slice(head * DIM, (head + 1) * DIM)
        at = slice(head, head + 1)
        entering = dot(query_ref[:, span], sum_ref[span, :].astype(bf16))
        student = inner_ref[:, span] + entering * reach[:, at]
        teacher = mean_ref[head] * shares[0][:, at]
        for k in range(3):
            teacher = teacher + means[k][head].astype(f32) * shares[1 + k][:, at]
        out_ref[:, span] = (
            student.astype(bf16).astype(f32) - teacher.astype(bf16).astype(f32)
        ).astype(bf16)


def finish(at, queries, decay, inner, own, means, states):
    return pl.pallas_call(
        finish_kernel,
        out_shape=jax.ShapeDtypeStruct((ROWS, HEADS * DIM), bf16),
        in_specs=[scalars] + [whole] * 13,
        out_specs=whole,
        scratch_shapes=[pltpu.VMEM((HEADS * DIM, DIM), f32)],
        compiler_params=params(),
        name="finish",
        cost_estimate=cost(5e7, 4e6, 1e5),
    )(at, queries, decay, inner, *own, *means, *states)


def project_kernel(at_ref, *refs):
    rows, weights = refs[:4], refs[4:13]
    sent_ref, kept_ref, stack_ref, held_ref, sems = refs[13:]
    depth = held_ref.shape[1]
    half = depth // 2
    copies = []
    for i, weight in enumerate(weights):
        if i < 7:
            source, target = weight.at[0:depth, :], held_ref.at[i]
        else:
            source, target = weight, held_ref.at[7, (i - 7) * half:(i - 6) * half, :]
        copies.append(pltpu.make_async_copy(source, target, sems.at[i]))
        copies[-1].start()
    for r in range(4):
        at = pl.multiple_of(at_ref[4 + r] * ROWS, ROWS)
        stack_ref[pl.ds(at, ROWS), :] = rows[r][...]
    for i in range(8):
        copies[i].wait()
        if i == 7:
            copies[8].wait()
        result = dot(stack_ref[...], held_ref[i]).astype(bf16)
        place, high = at_ref[i % 4], at_ref[8 + i // 4]
        for low in range(2):
            sent_ref[place, high, low] = result[low * ROWS:(low + 1) * ROWS]
            kept_ref[place, high, low] = result[(2 + low) * ROWS:(3 + low) * ROWS]


def project(at, rows, weights):
    depth, width = weights[0].shape
    out = jax.ShapeDtypeStruct((4, 2, 2, ROWS, width), bf16)
    return pl.pallas_call(
        project_kernel,
        out_shape=(out, out),
        in_specs=[scalars] + [whole] * 4 + [pl.BlockSpec(memory_space=pl.ANY)] * 9,
        out_specs=(whole, whole),
        scratch_shapes=[
            pltpu.VMEM((4 * ROWS, depth), bf16),
            pltpu.VMEM((8, depth, width), bf16),
            pltpu.SemaphoreType.DMA((9,)),
        ],
        compiler_params=params(),
        name="project",
        cost_estimate=cost(2 * 8 * 4 * ROWS * depth * width, 8e6),
    )(at, *rows, *weights)


Y = ("yh", "yl")
SEQ = ("x", "yh", "yl", "zh")
TP = ("zl", "c")


def moved(value, axis, by, count):
    return lax.ppermute(value, axis, [(i, (i + by) % count) for i in range(count)])


def shards(
    queries,
    cache_keys,
    prefix_values,
    slab_key_rows,
    slab_value_rows,
    student_log_decay,
    student_step,
    student_skip_weight,
    out_weight,
):
    x, yh, yl, zh = (lax.axis_index(a) for a in SEQ)
    zl, core = (lax.axis_index(a) for a in TP)
    y = yh * 2 + yl
    steps = (0, -1, 1, -2)

    def numbers(*values):
        return jnp.stack([jnp.asarray(v).astype(jnp.int32) for v in values])

    def around(value, axis):
        return [moved(value, axis, by, 4) for by in (1, 3, 2)]

    skip = student_skip_weight.reshape(1, HEADS)
    own, decay, step = pack(
        slab_key_rows, slab_value_rows, cache_keys, prefix_values, student_log_decay, student_step
    )
    other = moved(own, "zh", 1, 2)
    own_near = around(own, Y)
    own, bundle_query = lax.optimization_barrier((own, queries))
    bundled = around(bundle(bundle_query, out_weight), "x")
    inner = inner_block(queries, own, decay, step, skip)
    other, inner = lax.optimization_barrier((other, inner))
    other_near = around(other, Y)
    own_near[1], weight_mine = lax.optimization_barrier((own_near[1], out_weight))
    weight_other = moved(weight_mine, "zh", 1, 2)
    places = [((y + d) % 4) * 2 + zh for d in steps] + [((y + d) % 4) * 2 + 1 - zh for d in steps]
    keys, wide, state, weight, total = collect(
        numbers(*places), [own] + own_near + [other] + other_near
    )
    states = [
        lax.ppermute(state, "x", [(i, i + by) for i in range(4 - by)]) for by in (1, 2, 3)
    ]
    half = out_weight.shape[0] // 2

    def answer(index):
        place = (x + steps[1 + index]) % 4
        return attend_others(numbers(place > x), bundled[index], keys, wide, "attend")

    means = [answer(0)]
    means[0], bundled[1] = lax.optimization_barrier((means[0], bundled[1]))
    means.append(answer(1))
    means[1], bundled[2], weight_other = lax.optimization_barrier(
        (means[1], bundled[2], weight_other)
    )
    other_up, other_down = moved(weight_other, "x", 1, 4), moved(weight_other, "x", 3, 4)
    means.append(answer(2))
    means[2], own_query, *states = lax.optimization_barrier((means[2], queries, *states))
    mine = attend_own(numbers(y * 2 + zh), own_query, keys, wide, weight, total)
    means = [moved(mean, "x", back, 4) for mean, back in zip(means, (3, 1, 2))]
    mine, other_up, other_down = lax.optimization_barrier((mine, other_up, other_down))
    weights = [out_weight] + bundled + [
        weight_other,
        other_up,
        other_down,
        moved(other_up[:half], "x", 1, 4),
        moved(other_down[half:], "x", 3, 4),
    ]
    gap = finish(numbers(x, x - 1, x - 2, x - 3), queries, decay, inner, mine, means, states)

    gaps = [gap] + around(gap, Y)
    at = [(x + d - zl) % 4 for d in steps]
    row_places = [(y + d) % 4 for d in steps]
    at += [jnp.where(p // 2 == core, 2, 0) + p % 2 for p in row_places]
    at += [zh, 1 - zh]
    sent, kept = project(numbers(*at), gaps, weights)
    from_core = moved(sent, "c", 1, 2)
    sums = kept.astype(f32) + from_core.astype(f32)
    pieces = [moved(sums[s].astype(bf16), "zl", s, 4) for s in (1, 2, 3)]
    summed = sums[0] + pieces[0].astype(f32) + pieces[1].astype(f32) + pieces[2].astype(f32)
    summed = jnp.transpose(summed, (1, 2, 0, 3)).astype(bf16).reshape(2, ROWS, 2 * 256)
    same = lax.dynamic_index_in_dim(summed, yl, 0, False)
    cross = lax.dynamic_index_in_dim(summed, 1 - yl, 0, False)
    turn = ("c", "yh", "yl")
    pairs = [(h, w, k) for h in range(2) for w in range(2) for k in range(2)]
    same = lax.ppermute(
        same, turn, [(k * 4 + h * 2 + w, h * 4 + k * 2 + w) for h, w, k in pairs]
    )
    cross = lax.ppermute(
        cross, turn, [(k * 4 + h * 2 + w, h * 4 + k * 2 + 1 - w) for h, w, k in pairs]
    )
    return jnp.concatenate(
        [jnp.where(yl == 0, same, cross), jnp.where(yl == 0, cross, same)], 1
    )


def solution(mesh):
    devices = np.asarray(mesh.devices).reshape(4, 2, 4, 2, 2, 2)
    split = Mesh(devices, TP + SEQ)
    rows = P(SEQ, TP)
    heads = P(TP, SEQ)
    return jax.shard_map(
        shards,
        mesh=split,
        in_specs=(rows, rows, rows, rows, rows, heads, heads, P(TP), heads),
        out_specs=rows,
        check_vma=False,
    )
```
